256 devices in a mesh: sector: 16 (over y, x), box: 16 (over z, core).
Axes of the slice: x: 4, y: 4, z: 8, core: 2. Of those that a mesh axis runs over, the one named last changes fastest.
Arguments:
- positions: float32 [3, 16, 1024, 128], P(None, 'sector', 'box'), may hold values from -0.9 to 0.9
- strengths: float32 [3, 16, 1024, 128], P(None, 'sector', 'box'), may hold values from -6 to 6
- counts: int32 [16, 1024], P('sector', 'box'), may hold values from 1 to 128
- cross_slot: int32 [16, 4096], P('sector', 'box'), may hold values from 0 to 8191, as said below
- arrive_box: int32 [16, 4096], P('sector', 'box'), may hold values from 0 to 63
- il_source: int32 [16, 1024, 16], P('sector', 'box'), may hold values from 0 to 63
- il_class: int32 [16, 1024, 16], P('sector', 'box'), may hold values from 0 to 3
- m2m: bfloat16 [4, 441, 441], replicated, may hold values from -0.125 to 0.125
- m2l_leaf: bfloat16 [4, 441, 441], replicated, may hold values from -0.0625 to 0.0625
- tree_up: bfloat16 [2, 441, 441], replicated, may hold values from -0.21875 to 0.21875
- tree_m2l: bfloat16 [2, 441, 441], replicated, may hold values from -0.25 to 0.25
- m2l_sector: bfloat16 [15, 441, 441], replicated, may hold values from -0.078125 to 0.078125
Outputs:
- new_positions: float32 [3, 16, 1024, 128], P(None, 'sector', 'box')
- velocity: float32 [3, 16, 1024, 128], P(None, 'sector', 'box')
The draws below stay inside these ranges and needn't reach their ends.
Inputs may be any that keep to these rules, and one draw needn't show every extreme that they name: `cross_slot`: within one block's 256 entries the slot numbers are distinct; a slot beyond its box's count carries nothing.
All inputs are finite; a program needn't handle non-finite values.
Results may differ from the reference program's by a relative error of at most 0.006.
Values may be sent and summed in bfloat16 or wider, within the bound.
A program may use at most 128 MiB of HBM per device.

```python
import math
import jax
import jax.numpy as jnp
from jax import lax

TERMS = 21
COEF = 441
SLOTS = 128
LEVELS_DEV = 3
BOX_DEV = 64
CROSS_DEV = 256
IL = 16
NCLASS = 4
SECTORS = 16
BOXES = 1024
N_BOX = 16


def choose_slots(subkey):
    return jax.random.permutation(subkey, BOX_DEV * SLOTS)[:CROSS_DEV]


def draw_cross_slot(key, part):
    block_count = SECTORS * (BOXES // BOX_DEV)
    key_list = jax.random.split(key, block_count)
    chosen = jax.vmap(choose_slots)(key_list)
    return chosen.reshape(SECTORS, BOXES // BOX_DEV * CROSS_DEV).astype(jnp.int32)


def set_ends(values, rng, least, top_value):
    spot = [jax.random.randint(jax.random.fold_in(rng, axis), (), 0, length) for axis, length in enumerate(values.shape)]
    main_axis = values.shape.index(max(values.shape))
    neighbour = spot[:main_axis] + [(spot[main_axis] + 1) % values.shape[main_axis]] + spot[main_axis + 1:]
    return values.at[tuple(spot)].set(least).at[tuple(neighbour)].set(top_value)


def block_levels(own_key, extent, shards, low, top_value):
    def one(axis_at, blocks):
        steps = jax.random.uniform(jax.random.fold_in(jax.random.fold_in(own_key, 6), axis_at), (blocks,), jnp.float32, low / len(shards), top_value / len(shards))
        return jnp.repeat(jnp.exp(steps), extent[axis_at] // blocks).reshape((-1,) + (1,) * (len(extent) - axis_at - 1))

    loudness = one(*shards[0])
    for cut in shards[1:]:
        loudness = loudness * one(*cut)
    return loudness


def bell_draw(stream_key, extent, scale, limit, pieces=(), kind=jnp.bfloat16):
    level = block_levels(stream_key, extent, pieces, -0.22, 0.18) if pieces else 1.0
    values = jax.random.normal(stream_key, extent, jnp.float32) * scale * level
    return jnp.minimum(jnp.maximum(values, -limit), limit).astype(kind)


def setup_inputs(seed: int = 0) -> dict:
    streams_of = jax.random.split(jax.random.key(seed), 13)
    positions = jnp.clip(jax.random.uniform(streams_of[0], (3, SECTORS, BOXES, SLOTS), jnp.float32, -0.9, 0.9) * block_levels(streams_of[0], (3, SECTORS, BOXES, SLOTS), ((1, 16), (2, 16)), -0.4, 0.0), -0.9, 0.9)
    strengths = bell_draw(streams_of[1], (3, SECTORS, BOXES, SLOTS), 1.0, 6.0, ((1, 16), (2, 16)), jnp.float32)
    counts = set_ends(jax.random.randint(streams_of[2], (SECTORS, BOXES), 1, SLOTS + 1), jax.random.fold_in(streams_of[2], 1), 1, SLOTS).astype(jnp.int32)
    cross_slot = draw_cross_slot(jax.random.fold_in(streams_of[12], 71), 0)
    arrive_box = set_ends(jax.random.randint(streams_of[4], (SECTORS, N_BOX * CROSS_DEV), 0, BOX_DEV), jax.random.fold_in(streams_of[4], 1), 0, BOX_DEV - 1).astype(jnp.int32)
    il_source = set_ends(jax.random.randint(streams_of[5], (SECTORS, BOXES, IL), 0, BOX_DEV), jax.random.fold_in(streams_of[5], 1), 0, BOX_DEV - 1).astype(jnp.int32)
    il_class = set_ends(jax.random.randint(streams_of[6], (SECTORS, BOXES, IL), 0, NCLASS), jax.random.fold_in(streams_of[6], 1), 0, NCLASS - 1).astype(jnp.int32)
    m2m = bell_draw(streams_of[7], (4, COEF, COEF), (4 * COEF) ** -0.5, 0.125)
    m2l_leaf = bell_draw(streams_of[8], (NCLASS, COEF, COEF), (16 * COEF) ** -0.5, 0.0625)
    tree_up = bell_draw(streams_of[9], (2, COEF, COEF), (2 * COEF) ** -0.5, 0.21875)
    tree_m2l = bell_draw(streams_of[10], (2, COEF, COEF), COEF ** -0.5, 0.25)
    m2l_sector = bell_draw(streams_of[11], (SECTORS - 1, COEF, COEF), ((SECTORS - 1) * COEF) ** -0.5, 0.078125)
    return {"positions": positions, "strengths": strengths, "counts": counts, "cross_slot": cross_slot, "arrive_box": arrive_box, "il_source": il_source, "il_class": il_class, "m2m": m2m, "m2l_leaf": m2l_leaf, "tree_up": tree_up, "tree_m2l": tree_m2l, "m2l_sector": m2l_sector}


DELTA_SQ = 0.25
TIME_STEP = 0.02
INV_FOUR_PI = 1.0 / (4.0 * math.pi)
HIGHEST_PRECISION = lax.Precision.HIGHEST
OFFSETS = ((0.0, 0.0, 0.0), (0.0, 0.0, -2.0), (0.0, 0.0, 2.0), (-2.0, 0.0, 0.0), (2.0, 0.0, 0.0))

def chebyshev(coordinate):
    scaled = 0.5 * coordinate
    series = [jnp.ones_like(scaled), scaled]
    for order in range(2, TERMS):
        series.append(2.0 * scaled * series[-1] - series[-2])
    return jnp.stack(series[:TERMS])

def multipoles(cheb_a, cheb_b, weights):
    weighted = weights[:, None] * cheb_a[None]
    return jnp.einsum('cjnp,knp->ncjk', weighted, cheb_b, precision=HIGHEST_PRECISION)

def evaluate(local, cheb_a, cheb_b):
    shaped = local.reshape(local.shape[0], 3, TERMS, TERMS)
    partial_sum = jnp.einsum('ncjk,knp->cjnp', shaped, cheb_b, precision=HIGHEST_PRECISION)
    return lax.optimization_barrier(jnp.sum(partial_sum * cheb_a[None], axis=1)) / TERMS

def pair_velocity(target, source, weight, offset):
    delta_x = target[0][:, :, None] - (source[0][:, None, :] + offset[0])
    delta_y = target[1][:, :, None] - (source[1][:, None, :] + offset[1])
    delta_z = target[2][:, :, None] - (source[2][:, None, :] + offset[2])
    radius_sq = delta_x * delta_x + delta_y * delta_y + delta_z * delta_z + DELTA_SQ
    inverse = INV_FOUR_PI / (radius_sq * jnp.sqrt(radius_sq))
    weight_x = weight[0][:, None, :]
    weight_y = weight[1][:, None, :]
    weight_z = weight[2][:, None, :]
    speed_x = lax.optimization_barrier(jnp.sum(inverse * (weight_y * delta_z - weight_z * delta_y), axis=2))
    speed_y = lax.optimization_barrier(jnp.sum(inverse * (weight_z * delta_x - weight_x * delta_z), axis=2))
    speed_z = lax.optimization_barrier(jnp.sum(inverse * (weight_x * delta_y - weight_y * delta_x), axis=2))
    return jnp.stack([speed_x, speed_y, speed_z])

def near_velocity(places, weights):
    sectors, boxes, slots = (places.shape[1], places.shape[2], places.shape[3])
    stacked = jnp.concatenate([places, weights], axis=0)
    zero_box = jnp.zeros_like(stacked[:, :, :1])
    lower = jnp.concatenate([zero_box, stacked[:, :, :-1]], axis=2)
    upper = jnp.concatenate([stacked[:, :, 1:], zero_box], axis=2)
    sources = [stacked, lower, upper, jnp.roll(stacked, 1, axis=1), jnp.roll(stacked, -1, axis=1)]
    total_boxes = sectors * boxes
    block = math.gcd(total_boxes, 64)

    def arrange(array):
        return array.reshape(array.shape[0], total_boxes // block, block, slots).transpose(1, 0, 2, 3)
    inputs = (arrange(places),) + tuple((arrange(item) for item in sources))

    def block_velocity(items):
        summed = jnp.zeros_like(items[0])
        for index in range(5):
            summed = summed + pair_velocity(items[0], items[1 + index][:3], items[1 + index][3:], OFFSETS[index])
        return summed
    result = lax.map(block_velocity, inputs)
    return result.transpose(1, 0, 2, 3).reshape(3, sectors, boxes, slots)

def far_velocity(places, weights, arrival_terms, il_global, il_class, m2m, m2l_leaf, tree_up, tree_m2l, m2l_sector):
    sectors, boxes = (places.shape[1], places.shape[2])
    coef = TERMS * TERMS
    by_sector_places = places.transpose(1, 0, 2, 3)
    by_sector_weights = weights.transpose(1, 0, 2, 3)

    def leaf_side(items):
        place, weight, arrived = items
        cheb_a = chebyshev(place[0])
        cheb_b = chebyshev(place[1])
        return (multipoles(cheb_a, cheb_b, weight) + arrived).reshape(boxes, 3, coef).astype(jnp.bfloat16)
    leaf = lax.map(leaf_side, (by_sector_places, by_sector_weights, arrival_terms))
    m2m_wide = m2m.astype(jnp.float32)
    level = leaf
    for depth in range(LEVELS_DEV):
        grouped = level.reshape(sectors, -1, 4, 3, coef).astype(jnp.float32)
        level = jnp.einsum('sgocx,oxy->sgcy', grouped, m2m_wide).astype(jnp.bfloat16)
    groups = boxes // BOX_DEV
    depth_count = groups.bit_length() - 1
    up_wide = tree_up.astype(jnp.float32)
    tree_levels = [level]
    for depth in range(depth_count):
        paired = tree_levels[-1].reshape(sectors, -1, 2, 3, coef).astype(jnp.float32)
        merged = jnp.einsum('sncx,xy->sncy', paired[:, :, 0], up_wide[0]) + jnp.einsum('sncx,xy->sncy', paired[:, :, 1], up_wide[1])
        tree_levels.append(merged.astype(jnp.bfloat16))
    roots = tree_levels[-1][:, 0].astype(jnp.float32)
    sector_wide = m2l_sector.astype(jnp.float32)
    far_sum = jnp.zeros((sectors, 3, coef), jnp.float32)
    for distance in range(1, sectors):
        far_sum = far_sum + jnp.einsum('scx,xy->scy', jnp.roll(roots, -distance, axis=0), sector_wide[distance - 1])
    local = far_sum.astype(jnp.bfloat16)[:, None]
    cross_wide = tree_m2l.astype(jnp.float32)
    for depth in reversed(range(depth_count)):
        node_level = tree_levels[depth].reshape(sectors, -1, 2, 3, coef).astype(jnp.float32)
        parent = local.astype(jnp.float32)
        first = jnp.einsum('sncy,xy->sncx', parent, up_wide[0]) + jnp.einsum('sncx,xy->sncy', node_level[:, :, 1], cross_wide[0])
        second = jnp.einsum('sncy,xy->sncx', parent, up_wide[1]) + jnp.einsum('sncx,xy->sncy', node_level[:, :, 0], cross_wide[1])
        local = jnp.stack([first, second], axis=2).reshape(sectors, -1, 3, coef).astype(jnp.bfloat16)
    for depth in range(LEVELS_DEV - 1):
        local = jnp.einsum('sgcy,oxy->sgocx', local.astype(jnp.float32), m2m_wide).reshape(sectors, -1, 3, coef).astype(jnp.bfloat16)
    leaf_wide = m2l_leaf.astype(jnp.float32)

    def leaf_down(items):
        parent, leaf_terms, place, sources, classes = items
        child = jnp.einsum('gcy,oxy->gocx', parent.astype(jnp.float32), m2m_wide).reshape(boxes, 3, coef)
        gathered = leaf_terms.reshape(boxes, 3 * coef)[sources].astype(jnp.float32)
        class_hit = (classes[:, :, None] == jnp.arange(NCLASS, dtype=jnp.int32)[None, None, :]).astype(jnp.float32)
        presum = jnp.einsum('bic,bix->cbx', class_hit, gathered).astype(jnp.bfloat16)
        presum = presum.reshape(NCLASS, boxes * 3, coef).astype(jnp.float32)
        translated = jnp.einsum('cnx,cxy->ny', presum, leaf_wide).reshape(boxes, 3, coef)
        cheb_a = chebyshev(place[0])
        cheb_b = chebyshev(place[1])
        return evaluate(child + translated, cheb_a, cheb_b)
    speeds = lax.map(leaf_down, (local, leaf, by_sector_places, il_global, il_class))
    return speeds.transpose(1, 0, 2, 3)

def reference(positions, strengths, counts, cross_slot, arrive_box, il_source, il_class, m2m, m2l_leaf, tree_up, tree_m2l, m2l_sector):
    sectors, boxes, slots = (positions.shape[1], positions.shape[2], positions.shape[3])
    groups = boxes // BOX_DEV
    slot_ids = jnp.arange(slots, dtype=jnp.int32)
    present = (slot_ids[None, None, :] < counts[:, :, None]).astype(jnp.float32)
    crossing = cross_slot.reshape(sectors, groups, CROSS_DEV)
    flat_present = present.reshape(sectors, groups, BOX_DEV * slots)
    sector_ids = jnp.arange(sectors, dtype=jnp.int32)[:, None, None]
    group_ids = jnp.arange(groups, dtype=jnp.int32)[None, :, None]
    departed = jnp.zeros((sectors, groups, BOX_DEV * slots), jnp.float32).at[sector_ids, group_ids, crossing].set(1.0)
    live = (flat_present * (1.0 - departed)).reshape(sectors, boxes, slots)
    flat_places = positions.reshape(3, sectors, groups, BOX_DEV * slots)
    flat_strength = strengths.reshape(3, sectors, groups, BOX_DEV * slots)
    leave_places = jnp.take_along_axis(flat_places, crossing[None], axis=3)
    leave_present = jnp.take_along_axis(flat_present, crossing, axis=2)
    leave_weights = jnp.take_along_axis(flat_strength, crossing[None], axis=3) * leave_present[None]
    arrive_places = jnp.roll(leave_places, 1, axis=1).reshape(3, sectors, groups * CROSS_DEV)
    arrive_weights = jnp.roll(leave_weights, 1, axis=1).reshape(3, sectors, groups * CROSS_DEV)
    arrive_global = (group_ids * BOX_DEV + arrive_box.reshape(sectors, groups, CROSS_DEV)).reshape(sectors, groups * CROSS_DEV)

    def arrival_side(items):
        place, weight, landing = items
        cheb_a = chebyshev(place[0][:, None])
        cheb_b = chebyshev(place[1][:, None])
        each = multipoles(cheb_a, cheb_b, weight[:, :, None])
        return jax.ops.segment_sum(each, landing, num_segments=boxes)
    arrival_terms = lax.map(arrival_side, (arrive_places.transpose(1, 0, 2), arrive_weights.transpose(1, 0, 2), arrive_global))
    box_base = (jnp.arange(boxes, dtype=jnp.int32) // BOX_DEV * BOX_DEV)[None, :, None]
    il_global = box_base + il_source
    weights = strengths * live[None]
    places = positions
    velocity = jnp.zeros_like(positions)
    for substep in range(2):
        near = near_velocity(places, weights)
        far = far_velocity(places, weights, arrival_terms, il_global, il_class, m2m, m2l_leaf, tree_up, tree_m2l, m2l_sector)
        velocity = near + far
        places = places + TIME_STEP * velocity
    return (places, velocity)
```

```python
import functools
import math

import jax
import jax.numpy as jnp
from jax import lax
from jax.experimental import pallas as pl
from jax.experimental.pallas import tpu as pltpu
from jax.sharding import PartitionSpec as P

TERMS = 21
COEF = TERMS * TERMS
PAD = 24
ROWS = 512
BOXES = 64
SLOTS = 128
CROSS = 256
NCLASS = 4
GROUP = 16
DELTA_SQ = 0.25
TIME_STEP = 0.02
INV_FOUR_PI = 1.0 / (4.0 * math.pi)
OFFSETS = ((0.0, 0.0, 0.0), (0.0, 0.0, -2.0), (0.0, 0.0, 2.0), (-2.0, 0.0, 0.0), (2.0, 0.0, 0.0))
BF16 = jnp.bfloat16
F32 = jnp.float32
MESH = pl.DeviceIdType.MESH

NN = (((1,), (0,)), ((), ()))
NT = (((1,), (1,)), ((), ()))


def mm(a, b):
    return lax.dot_general(a, b, NN, preferred_element_type=F32)


def mm_t(a, b):
    return lax.dot_general(a, b, NT, preferred_element_type=F32)


def rounded(value):
    return value.astype(BF16).astype(F32)


def iota(shape, dim):
    return lax.broadcasted_iota(jnp.int32, shape, dim)


def one_where(condition, dtype=F32):
    return jnp.where(condition, 1.0, 0.0).astype(dtype)


def reversed_digits(index):
    return (index & 3) * 16 + ((index >> 2) & 3) * 4 + (index >> 4)


def kernel(
    pos_ref, str_ref, cnt_ref, cross_ref, arr_ref, ils_ref, ilc_ref,
    m2m_hbm, m2l_hbm, up_hbm, tm_hbm, sec_hbm,
    outp_ref, outv_ref,
    m2m, m2l, up, tm, sec,
    weights, places, halo_p, halo_w, end_out, end_in, leave_out, leave_in,
    src_f, src_s, tgt_f, cheb_a, cheb_b, arr_a, arr_b, phi_ref,
    leaf_box, local_box, near_box, far_box,
    arr_leaf, leaf504, leaf441, select, counts_pc, presum, translated,
    up1, up2, root, pack_f, root_out, root_in, tree_e, tree_o, down1, down2, down3,
    sec_out, sec_in,
    load_sem, send_sem, recv_sem,
):
    s_id = lax.axis_index("sector")
    g_id = lax.axis_index("box")

    loads = []
    for index, (src, dst) in enumerate(((m2m_hbm, m2m), (up_hbm, up), (m2l_hbm, m2l), (tm_hbm, tm), (sec_hbm, sec))):
        copy = pltpu.make_async_copy(src, dst, load_sem.at[index])
        copy.start()
        loads.append(copy)

    def box_peer(distance):
        total = 0
        for bit in range(4):
            mine = (g_id // (1 << bit)) % 2
            total = total + ((mine + (distance >> bit & 1)) % 2) * (1 << bit)
        return (s_id, total)

    def sector_peer(distance):
        return ((s_id + distance) % GROUP, g_id)

    barrier = pltpu.get_barrier_semaphore()
    for distance in range(1, GROUP):
        pl.semaphore_signal(barrier, inc=1, device_id=box_peer(distance), device_id_type=MESH)
        pl.semaphore_signal(barrier, inc=1, device_id=sector_peer(distance), device_id_type=MESH)
    before = (s_id, (g_id + GROUP - 1) % GROUP)
    after = (s_id, (g_id + 1) % GROUP)

    next_sem = [0]
    sends = []

    def remote(src, dst, device):
        index = next_sem[0]
        next_sem[0] += 1
        copy = pltpu.make_async_remote_copy(
            src_ref=src, dst_ref=dst, send_sem=send_sem.at[index], recv_sem=recv_sem.at[index],
            device_id=device, device_id_type=MESH,
        )
        copy.start()
        sends.append(copy)
        return copy

    diagonal = iota((BOXES, BOXES), 0) == iota((BOXES, BOXES), 1)
    count_col = jnp.sum(jnp.where(diagonal, jnp.broadcast_to(cnt_ref[...].astype(F32), (BOXES, BOXES)), 0.0), axis=1, keepdims=True)
    present = one_where(iota((BOXES, SLOTS), 1).astype(F32) < count_col)
    crossing = cross_ref[...]
    hit_box = one_where(iota((BOXES, CROSS), 0) == (crossing >> 7), BF16)
    hit_slot = one_where(iota((SLOTS, CROSS), 0) == (crossing & 127))
    departed = mm_t(hit_box, hit_slot.astype(BF16))
    live = present * (1.0 - departed)
    leave_out[...] = jnp.zeros_like(leave_out)
    for c in range(3):
        weights[c] = str_ref[c] * live
    for c in range(6):
        value = pos_ref[c] if c < 3 else str_ref[c - 3] * present
        turned = value.T
        high = turned.astype(BF16)
        rest = turned - high.astype(F32)
        middle = rest.astype(BF16)
        low = (rest - middle.astype(F32)).astype(BF16)
        picked = mm(high, hit_box) + mm(middle, hit_box) + mm(low, hit_box)
        leave_out[c : c + 1, :] = jnp.sum(picked * hit_slot, axis=0, keepdims=True)

    def fill_ends(step, place):
        end_out[step] = jnp.zeros((2, 8, SLOTS), F32)
        for c in range(3):
            end_out[step, 0, c : c + 1, :] = place[c, BOXES - 1 : BOXES, :]
            end_out[step, 1, c : c + 1, :] = place[c, 0:1, :]
            end_out[step, 0, 3 + c : 4 + c, :] = weights[c, BOXES - 1 : BOXES, :]
            end_out[step, 1, 3 + c : 4 + c, :] = weights[c, 0:1, :]

    fill_ends(0, pos_ref)
    pl.semaphore_wait(barrier, 2 * (GROUP - 1))
    got_leave = remote(leave_out, leave_in, sector_peer(1))

    def send_halo(step, place):
        return [
            remote(place, halo_p.at[step, 0], sector_peer(1)),
            remote(place, halo_p.at[step, 1], sector_peer(GROUP - 1)),
            remote(end_out.at[step, 0], end_in.at[step, 0], after),
            remote(end_out.at[step, 1], end_in.at[step, 1], before),
        ]

    got_weights = [
        remote(weights, halo_w.at[0], sector_peer(1)),
        remote(weights, halo_w.at[1], sector_peer(GROUP - 1)),
    ]
    got_halo = send_halo(0, pos_ref)

    row = iota((ROWS, ROWS), 0)
    order = (row * 2731) >> 16
    select[...] = one_where((iota((ROWS, ROWS), 1) == row - 3 * order) & (row - PAD * order < TERMS) & (order < TERMS), BF16)
    for ref in (cheb_a, cheb_b, arr_a, arr_b, up1, up2, root, pack_f, tree_e, tree_o, down1, down2, local_box):
        ref[...] = jnp.zeros_like(ref)

    permute = one_where(reversed_digits(iota((BOXES, BOXES), 0)) == iota((BOXES, BOXES), 1), BF16)
    code = mm(permute, (ils_ref[...] + BOXES * ilc_ref[...]).astype(F32).astype(BF16))
    source = reversed_digits(iota((BOXES, BOXES), 1)).astype(F32)
    for kind in range(NCLASS):
        wanted = source + float(BOXES * kind)
        total = jnp.zeros((BOXES, BOXES), F32)
        for entry in range(16):
            total = total + one_where(code[:, entry : entry + 1] == wanted)
        counts_pc[kind * BOXES : (kind + 1) * BOXES, :] = total.astype(BF16)

    def split(value):
        high = rounded(value)
        return high, value - high

    def put_targets(x, y, z):
        rows = []
        halves = [split(v) for v in (x, y, z)]
        rows += [h for h, _ in halves] * 2 + [l for _, l in halves]
        norm = x * x + y * y + z * z
        n1, rest = split(norm)
        n2, n3 = split(rest)
        rows += [n1, n2, n3]
        for index, value in enumerate(rows):
            tgt_f[pl.ds(index, BOXES, stride=16), :] = value

    def put_sources(kind, base, count, coords, weight):
        offset = OFFSETS[kind]
        x, y, z = (v + o if o else v for v, o in zip(coords, offset))
        halves = [split(-2.0 * v) for v in (x, y, z)]
        highs = [h for h, _ in halves]
        m1, rest = split(x * x + y * y + z * z + DELTA_SQ)
        m2, m3 = split(rest)
        ones = jnp.ones_like(x)
        rows = highs + [l for _, l in halves] + highs + [ones] * 3 + [m1, m2, m3, jnp.zeros_like(x)]
        wx, wy, wz = weight
        moments = [wx, wy, wz, wy * z - wz * y, wz * x - wx * z, wx * y - wy * x]
        parts = [split(v) for v in moments]
        zero = jnp.zeros_like(x)
        sums = [h for h, _ in parts] + [zero] * 2 + [l for _, l in parts] + [zero] * 2
        for index in range(16):
            if count == 1:
                spot = slice(base * 16 + index, base * 16 + index + 1)
            else:
                spot = pl.ds(base * 16 + index, count, stride=16)
            src_f[kind, spot, :] = rows[index]
            src_s[kind, spot, :] = sums[index]

    for index in range(12, 16):
        tgt_f[pl.ds(index, BOXES, stride=16), :] = jnp.full((BOXES, SLOTS), 1.0 if index < 15 else 0.0, F32)

    def series(coordinate, put):
        scaled = 0.5 * coordinate
        older, newer = jnp.ones_like(scaled), scaled
        put(0, older)
        put(1, newer)
        for index in range(2, TERMS):
            older, newer = newer, 2.0 * scaled * newer - older
            put(index, newer)

    def own_terms(place):
        x, y, z = place[0], place[1], place[2]
        weight = (weights[0], weights[1], weights[2])
        put_targets(x, y, z)
        put_sources(0, 0, BOXES, (x, y, z), weight)
        put_sources(1, 1, BOXES, (x, y, z), weight)
        put_sources(2, 0, BOXES, (x, y, z), weight)

        def put_a(index, value):
            cheb_a[pl.ds(index, BOXES, stride=PAD), :] = value

        def put_b(index, value):
            cheb_b[pl.ds(index, BOXES, stride=PAD), :] = value

        series(x, put_a)
        series(y, put_b)

    def halo_terms(step):
        for side in range(2):
            got_halo[side].wait_recv()
            if step == 0:
                got_weights[side].wait_recv()
            coords = tuple(halo_p[step, side, c] for c in range(3))
            weight = tuple(halo_w[side, c] for c in range(3))
            put_sources(3 + side, 0, BOXES, coords, weight)
        for side in range(2):
            got_halo[2 + side].wait_recv()
            inside = (g_id > 0) if side == 0 else (g_id < GROUP - 1)
            keep = jnp.where(inside, 1.0, 0.0).astype(F32)
            coords = tuple(end_in[step, side, c : c + 1, :] for c in range(3))
            weight = tuple(end_in[step, side, 3 + c : 4 + c, :] * keep for c in range(3))
            put_sources(1 + side, 0 if side == 0 else BOXES, 1, coords, weight)

    def basis(a_row, b_block, width):
        pieces = []
        for index in range(0, TERMS - 1, 2):
            pair = jnp.concatenate([a_row(index) * b_block, a_row(index + 1) * b_block], axis=0)
            pieces.append(pair.astype(BF16))
        last = jnp.concatenate([a_row(TERMS - 1) * b_block, jnp.zeros((8, width), F32)], axis=0)
        pieces.append(last.astype(BF16))
        return jnp.concatenate(pieces, axis=0)

    def box_order(box):
        return (box % 4) * 16 + ((box // 4) % 4) * 4 + box // 16

    def leaf_step(box, carry):
        start = pl.multiple_of(box * PAD, 8)
        b_block = cheb_b[pl.ds(start, PAD), :]
        phi = basis(lambda j: cheb_a[pl.ds(start + j, 1), :], b_block, SLOTS)
        phi_ref[box] = phi
        lhs = src_s[0, pl.ds(pl.multiple_of(box * 16, 16), 16), :].astype(BF16)
        got = mm_t(lhs, phi)
        got = got[0:8] + got[8:16]
        spot = pl.ds(pl.multiple_of(box_order(box) * 8, 8), 8)
        for t in range(4):
            leaf_box[t, spot, :] = got[:, t * 128 : (t + 1) * 128]
        return carry

    def arrival_terms():
        got_leave.wait_recv()

        def put_a(index, value):
            arr_a[index : index + 1, :] = value

        def put_b(index, value):
            arr_b[index : index + 1, :] = value

        series(leave_in[0:1, :], put_a)
        series(leave_in[1:2, :], put_b)
        phi = basis(lambda j: arr_a[j : j + 1, :], arr_b[...], CROSS)
        landing = one_where(reversed_digits(iota((BOXES, CROSS), 0)) == arr_ref[...])
        for c in range(3):
            high, low = split(landing * leave_in[3 + c : 4 + c, :])
            arr_leaf[c * BOXES : (c + 1) * BOXES, :] = mm_t(high.astype(BF16), phi) + mm_t(low.astype(BF16), phi)

    def make_leaf():
        for c in range(3):
            rows = slice(c * BOXES, (c + 1) * BOXES)
            for t in range(4):
                lanes = slice(t * 128, (t + 1) * 128)
                own = leaf_box[t, pl.ds(c, BOXES, stride=8), :]
                leaf504[rows, lanes] = (own + arr_leaf[rows, lanes]).astype(BF16)
        leaf441[...] = mm(leaf504[...], select[...]).astype(BF16)

    def pack(value, out):
        root[:, 0:COEF] = value
        for t in range(4):
            pack_f[t * 4 : t * 4 + 3, :] = root[0:3, t * 128 : (t + 1) * 128]
        out[...] = pack_f[...].astype(BF16)

    def upward():
        total = None
        for o in range(4):
            lhs = jnp.concatenate([leaf441[c * BOXES + o * 16 : c * BOXES + o * 16 + 16, 0:COEF] for c in range(3)], axis=0)
            part = mm(lhs, m2m[o])
            total = part if total is None else total + part
        level = rounded(total)
        for o in range(4):
            for c in range(3):
                up1[o, c * 4 : c * 4 + 4, 0:COEF] = level[c * 16 + o * 4 : c * 16 + o * 4 + 4]
        total = None
        for o in range(4):
            part = mm(up1[o, :, 0:COEF].astype(BF16), m2m[o])
            total = part if total is None else total + part
        level = rounded(total)
        for o in range(4):
            for c in range(3):
                up2[o, c : c + 1, 0:COEF] = level[c * 4 + o : c * 4 + o + 1]
        total = None
        for o in range(4):
            part = mm(up2[o, :, 0:COEF].astype(BF16), m2m[o])
            total = part if total is None else total + part
        return total

    def bit(level):
        return (g_id // (1 << level)) % 2

    def spread(index, ref, spot):
        value = ref[index].astype(F32)
        for t in range(4):
            spot[0][spot[1] * 4 : spot[1] * 4 + 4, t * 128 : (t + 1) * 128] = value[t * 4 : t * 4 + 4]

    def tree(step):
        for distance in range(GROUP):
            half = distance // 2
            spot = (half & 1) * 4 + (half >> 1 & 1) * 2 + (half >> 2)
            spread(distance, root_in.at[step], (tree_o if distance & 1 else tree_e, spot))
        lower = tree_e[:, 0:COEF].astype(BF16)
        upper = tree_o[:, 0:COEF].astype(BF16)
        siblings = []
        for level in range(4):
            siblings.append(upper[0:8] if upper.shape[0] >= 8 else upper)
            merged = mm(lower, up[bit(level)]) + mm(upper, up[1 - bit(level)])
            if level < 3:
                half = merged.shape[0] // 2
                lower = merged[0:half].astype(BF16)
                upper = merged[half:].astype(BF16)
        return merged, siblings

    def translate():
        for c in range(3):
            got = mm(counts_pc[...], leaf441[c * BOXES : (c + 1) * BOXES, :]).astype(BF16)
            for kind in range(NCLASS):
                presum[kind, c * BOXES : (c + 1) * BOXES, :] = got[kind * BOXES : (kind + 1) * BOXES]
        total = None
        for kind in range(NCLASS):
            part = mm(presum[kind, :, 0:COEF], m2l[kind])
            total = part if total is None else total + part
        translated[:, 0:COEF] = total

    def near_step(box, carry):
        own = pl.ds(pl.multiple_of(box * 16, 16), 16)
        later = pl.ds(pl.multiple_of(box * 16 + 16, 16), 16)
        target = tgt_f[own, :].T.astype(BF16)
        total = jnp.zeros((16, SLOTS), F32)
        for kind in range(5):
            spot = later if kind == 2 else own
            radius_sq = mm(target, src_f[kind, spot, :].astype(BF16))
            inverse = lax.rsqrt(radius_sq)
            cubed = (inverse * inverse * inverse).astype(BF16)
            total = total + mm_t(src_s[kind, spot, :].astype(BF16), cubed)
        near_box[pl.ds(pl.multiple_of(box * 8, 8), 8), :] = total[0:8] + total[8:16]
        return carry

    def downward(local):
        local = local.astype(BF16)
        for o in range(4):
            part = rounded(mm_t(local, m2m[o]))
            for c in range(3):
                down1[c * 4 + o : c * 4 + o + 1, 0:COEF] = part[c : c + 1]
        level = down1[:, 0:COEF].astype(BF16)
        for o in range(4):
            part = rounded(mm_t(level, m2m[o]))
            for c in range(3):
                down2[c * 16 + o * 4 : c * 16 + o * 4 + 4, 0:COEF] = part[c * 4 : c * 4 + 4]
        level = down2[:, 0:COEF].astype(BF16)
        for o in range(4):
            part = mm_t(level, m2m[o])
            for c in range(3):
                rows = slice(c * BOXES + o * 16, c * BOXES + o * 16 + 16)
                down3[rows, 0:COEF] = part[c * 16 : c * 16 + 16] + translated[rows, 0:COEF]
        high, low = split(down3[:, 0:COEF])
        chosen = select[:, 0:COEF]
        final = mm_t(high.astype(BF16), chosen) + mm_t(low.astype(BF16), chosen)
        for c in range(3):
            for t in range(4):
                local_box[t, pl.ds(c, BOXES, stride=8), :] = final[c * BOXES : (c + 1) * BOXES, t * 128 : (t + 1) * 128]

    def far_step(box, carry):
        spot = pl.ds(pl.multiple_of(box_order(box) * 8, 8), 8)
        value = jnp.concatenate([local_box[t, spot, :] for t in range(4)], axis=1)
        high, low = split(value)
        lhs = jnp.concatenate([high, low], axis=0).astype(BF16)
        got = mm(lhs, phi_ref[box])
        far_box[pl.ds(pl.multiple_of(box * 8, 8), 8), :] = got[0:8] + got[8:16]
        return carry

    for step in range(2):
        place = pos_ref if step == 0 else places
        if step == 1:
            fill_ends(1, places)
            got_halo = send_halo(1, places)
        own_terms(place)
        lax.fori_loop(0, BOXES, leaf_step, 0)
        if step == 0:
            arrival_terms()
            loads[0].wait()
        make_leaf()
        pack(upward(), root_out.at[step])
        root_in[step, 0] = root_out[step]
        got_roots = [
            remote(root_out.at[step], root_in.at[step, distance], box_peer(distance)) for distance in range(1, GROUP)
        ]
        if step == 0:
            for copy in loads[1:]:
                copy.wait()
        translate()
        halo_terms(step)
        lax.fori_loop(0, BOXES // 2, near_step, 0)
        for copy in got_roots:
            copy.wait_recv()
        top, siblings = tree(step)
        pack(jnp.concatenate([top, jnp.zeros((4, COEF), F32)], axis=0), sec_out.at[step])
        got_sectors = [
            remote(sec_out.at[step], sec_in.at[step, distance - 1], sector_peer(distance)) for distance in range(1, GROUP)
        ]
        crossed = [mm(siblings[level], tm[bit(level)])[0:4] for level in range(4)]
        lax.fori_loop(BOXES // 2, BOXES, near_step, 0)
        for copy in got_sectors:
            copy.wait_recv()
        total = jnp.zeros((4, COEF), F32)
        for distance in range(1, GROUP):
            spread(distance - 1, sec_in.at[step], (root, 0))
            total = total + mm(root[0:4, 0:COEF].astype(BF16), sec[GROUP - 1 - distance])
        local = total
        for level in reversed(range(4)):
            local = mm_t(local.astype(BF16), up[bit(level)]) + crossed[level]
        downward(local)
        lax.fori_loop(0, BOXES, far_step, 0)
        near = [near_box[pl.ds(c, BOXES, stride=8), :] for c in range(6)]
        x, y, z = place[0], place[1], place[2]
        swept = (
            near[1] * z - near[2] * y - near[3],
            near[2] * x - near[0] * z - near[4],
            near[0] * y - near[1] * x - near[5],
        )
        for c in range(3):
            velocity = INV_FOUR_PI * swept[c] + far_box[pl.ds(c, BOXES, stride=8), :] / float(TERMS)
            if step == 0:
                places[c] = place[c] + TIME_STEP * velocity
            else:
                outp_ref[c] = place[c] + TIME_STEP * velocity
                outv_ref[c] = velocity

    for copy in sends:
        copy.wait_send()


def per_device(positions, strengths, counts, cross_slot, arrive_box, il_source, il_class, m2m, m2l_leaf, tree_up, tree_m2l, m2l_sector):
    vmem = pl.BlockSpec(memory_space=pltpu.VMEM)
    hbm = pl.BlockSpec(memory_space=pl.ANY)
    block = jax.ShapeDtypeStruct((3, BOXES, SLOTS), F32)
    scratch = [
        pltpu.VMEM((4, COEF, COEF), BF16),
        pltpu.VMEM((4, COEF, COEF), BF16),
        pltpu.VMEM((2, COEF, COEF), BF16),
        pltpu.VMEM((2, COEF, COEF), BF16),
        pltpu.VMEM((15, COEF, COEF), BF16),
        pltpu.VMEM((3, BOXES, SLOTS), F32),
        pltpu.VMEM((3, BOXES, SLOTS), F32),
        pltpu.VMEM((2, 2, 3, BOXES, SLOTS), F32),
        pltpu.VMEM((2, 3, BOXES, SLOTS), F32),
        pltpu.VMEM((2, 2, 8, SLOTS), F32),
        pltpu.VMEM((2, 2, 8, SLOTS), F32),
        pltpu.VMEM((8, CROSS), F32),
        pltpu.VMEM((8, CROSS), F32),
        pltpu.VMEM((5, (BOXES + 1) * 16, SLOTS), F32),
        pltpu.VMEM((5, (BOXES + 1) * 16, SLOTS), F32),
        pltpu.VMEM((BOXES * 16, SLOTS), F32),
        pltpu.VMEM((BOXES * PAD, SLOTS), F32),
        pltpu.VMEM((BOXES * PAD, SLOTS), F32),
        pltpu.VMEM((PAD, CROSS), F32),
        pltpu.VMEM((PAD, CROSS), F32),
        pltpu.VMEM((BOXES, ROWS, SLOTS), BF16),
        pltpu.VMEM((4, BOXES * 8, SLOTS), F32),
        pltpu.VMEM((4, BOXES * 8, SLOTS), F32),
        pltpu.VMEM((BOXES * 8, SLOTS), F32),
        pltpu.VMEM((BOXES * 8, SLOTS), F32),
        pltpu.VMEM((3 * BOXES, ROWS), F32),
        pltpu.VMEM((3 * BOXES, ROWS), BF16),
        pltpu.VMEM((3 * BOXES, ROWS), BF16),
        pltpu.VMEM((ROWS, ROWS), BF16),
        pltpu.VMEM((NCLASS * BOXES, BOXES), BF16),
        pltpu.VMEM((NCLASS, 3 * BOXES, ROWS), BF16),
        pltpu.VMEM((3 * BOXES, ROWS), F32),
        pltpu.VMEM((4, 16, ROWS), F32),
        pltpu.VMEM((4, 8, ROWS), F32),
        pltpu.VMEM((8, ROWS), F32),
        pltpu.VMEM((16, SLOTS), F32),
        pltpu.VMEM((2, 16, SLOTS), BF16),
        pltpu.VMEM((2, GROUP, 16, SLOTS), BF16),
        pltpu.VMEM((32, ROWS), F32),
        pltpu.VMEM((32, ROWS), F32),
        pltpu.VMEM((16, ROWS), F32),
        pltpu.VMEM((48, ROWS), F32),
        pltpu.VMEM((3 * BOXES, ROWS), F32),
        pltpu.VMEM((2, 16, SLOTS), BF16),
        pltpu.VMEM((2, GROUP - 1, 16, SLOTS), BF16),
        pltpu.SemaphoreType.DMA((5,)),
        pltpu.SemaphoreType.DMA((72,)),
        pltpu.SemaphoreType.DMA((72,)),
    ]
    new_places, velocity = pl.pallas_call(
        kernel,
        out_shape=(block, block),
        in_specs=[vmem] * 7 + [hbm] * 5,
        out_specs=(vmem, vmem),
        scratch_shapes=scratch,
        compiler_params=pltpu.CompilerParams(
            collective_id=0, has_side_effects=True, vmem_limit_bytes=52 * 1024 * 1024
        ),
        name="vortex_wake",
    )(
        positions[:, 0], strengths[:, 0], counts, cross_slot, arrive_box, il_source[0], il_class[0],
        m2m, m2l_leaf, tree_up, tree_m2l, m2l_sector,
    )
    return new_places[:, None], velocity[:, None]


def solution(mesh):
    placed = (
        P(None, "sector", "box", None),
        P(None, "sector", "box", None),
        P("sector", "box"),
        P("sector", "box"),
        P("sector", "box"),
        P("sector", "box", None),
        P("sector", "box", None),
        P(),
        P(),
        P(),
        P(),
        P(),
    )
    return jax.shard_map(
        per_device,
        mesh=mesh,
        in_specs=placed,
        out_specs=(P(None, "sector", "box", None), P(None, "sector", "box", None)),
        check_vma=False,
    )
```

```python
import functools
import math

import jax
import jax.numpy as jnp
from jax import lax
from jax.experimental import pallas as pl
from jax.experimental.pallas import tpu as pltpu
from jax.sharding import PartitionSpec as P

TERMS = 21
COEF = TERMS * TERMS
PAD = 24
ROWS = 512
BOXES = 64
SLOTS = 128
CROSS = 256
NCLASS = 4
GROUP = 16
LEAF_PER = 8
NEAR_PER = 8
FAR_PER = 8
DELTA_SQ = 0.25
TIME_STEP = 0.02
INV_FOUR_PI = 1.0 / (4.0 * math.pi)
OFFSETS = ((0.0, 0.0, 0.0), (0.0, 0.0, -2.0), (0.0, 0.0, 2.0), (-2.0, 0.0, 0.0), (2.0, 0.0, 0.0))
BF16 = jnp.bfloat16
F32 = jnp.float32
MESH = pl.DeviceIdType.MESH

NN = (((1,), (0,)), ((), ()))
NT = (((1,), (1,)), ((), ()))


def mm(a, b):
    return lax.dot_general(a, b, NN, preferred_element_type=F32)


def mm_t(a, b):
    return lax.dot_general(a, b, NT, preferred_element_type=F32)


def rounded(value):
    return value.astype(BF16).astype(F32)


def iota(shape, dim):
    return lax.broadcasted_iota(jnp.int32, shape, dim)


def one_where(condition, dtype=F32):
    return jnp.where(condition, 1.0, 0.0).astype(dtype)


def reversed_digits(index):
    return (index & 3) * 16 + ((index >> 2) & 3) * 4 + (index >> 4)


def kernel(
    pos_ref, str_ref, cnt_ref, cross_ref, arr_ref, ils_ref, ilc_ref,
    m2m_hbm, m2l_hbm, up_hbm, tm_hbm, sec_hbm,
    outp_ref, outv_ref,
    m2m, m2l, up, tm, sec,
    weights, places, halo_p, halo_w, end_out, end_in, leave_out, leave_in,
    src_f, src_s, tgt_f, cheb_a, cheb_b, arr_a, arr_b, phi_ref,
    leaf_box, local_box, near_box, far_box,
    arr_leaf, leaf504, leaf441, select, counts_pc, presum, translated,
    up1, up2, root, pack_f, root_out, root_in, tree_e, tree_o, down1, down2, down3,
    sec_out, sec_in,
    load_sem, send_sem, recv_sem,
):
    s_id = lax.axis_index("sector")
    g_id = lax.axis_index("box")

    loads = []
    for index, (src, dst) in enumerate(((m2m_hbm, m2m), (up_hbm, up), (m2l_hbm, m2l), (tm_hbm, tm), (sec_hbm, sec))):
        copy = pltpu.make_async_copy(src, dst, load_sem.at[index])
        copy.start()
        loads.append(copy)

    def box_peer(distance):
        total = 0
        for bit in range(4):
            mine = (g_id // (1 << bit)) % 2
            total = total + ((mine + (distance >> bit & 1)) % 2) * (1 << bit)
        return (s_id, total)

    def sector_peer(distance):
        return ((s_id + distance) % GROUP, g_id)

    barrier = pltpu.get_barrier_semaphore()
    for distance in range(1, GROUP):
        pl.semaphore_signal(barrier, inc=1, device_id=box_peer(distance), device_id_type=MESH)
        pl.semaphore_signal(barrier, inc=1, device_id=sector_peer(distance), device_id_type=MESH)
    before = (s_id, (g_id + GROUP - 1) % GROUP)
    after = (s_id, (g_id + 1) % GROUP)

    next_sem = [0]
    sends = []

    def remote(src, dst, device):
        index = next_sem[0]
        next_sem[0] += 1
        copy = pltpu.make_async_remote_copy(
            src_ref=src, dst_ref=dst, send_sem=send_sem.at[index], recv_sem=recv_sem.at[index],
            device_id=device, device_id_type=MESH,
        )
        copy.start()
        sends.append(copy)
        return copy

    diagonal = iota((BOXES, BOXES), 0) == iota((BOXES, BOXES), 1)
    count_col = jnp.sum(jnp.where(diagonal, jnp.broadcast_to(cnt_ref[...].astype(F32), (BOXES, BOXES)), 0.0), axis=1, keepdims=True)
    present = one_where(iota((BOXES, SLOTS), 1).astype(F32) < count_col)
    crossing = cross_ref[...]
    hit_box = one_where(iota((BOXES, CROSS), 0) == (crossing >> 7), BF16)
    hit_slot = one_where(iota((SLOTS, CROSS), 0) == (crossing & 127))
    departed = mm_t(hit_box, hit_slot.astype(BF16))
    live = present * (1.0 - departed)
    leave_out[...] = jnp.zeros_like(leave_out)
    for c in range(3):
        weights[c] = str_ref[c] * live
    for c in range(6):
        value = pos_ref[c] if c < 3 else str_ref[c - 3] * present
        turned = value.T
        high = turned.astype(BF16)
        rest = turned - high.astype(F32)
        middle = rest.astype(BF16)
        low = (rest - middle.astype(F32)).astype(BF16)
        picked = mm(high, hit_box) + mm(middle, hit_box) + mm(low, hit_box)
        leave_out[c : c + 1, :] = jnp.sum(picked * hit_slot, axis=0, keepdims=True)

    def fill_ends(step, place):
        end_out[step] = jnp.zeros((2, 8, SLOTS), F32)
        for c in range(3):
            end_out[step, 0, c : c + 1, :] = place[c, BOXES - 1 : BOXES, :]
            end_out[step, 1, c : c + 1, :] = place[c, 0:1, :]
            end_out[step, 0, 3 + c : 4 + c, :] = weights[c, BOXES - 1 : BOXES, :]
            end_out[step, 1, 3 + c : 4 + c, :] = weights[c, 0:1, :]

    fill_ends(0, pos_ref)
    pl.semaphore_wait(barrier, 2 * (GROUP - 1))
    got_leave = remote(leave_out, leave_in, sector_peer(1))

    def send_halo(step, place):
        return [
            remote(place, halo_p.at[step, 0], sector_peer(1)),
            remote(place, halo_p.at[step, 1], sector_peer(GROUP - 1)),
            remote(end_out.at[step, 0], end_in.at[step, 0], after),
            remote(end_out.at[step, 1], end_in.at[step, 1], before),
        ]

    got_weights = [
        remote(weights, halo_w.at[0], sector_peer(1)),
        remote(weights, halo_w.at[1], sector_peer(GROUP - 1)),
    ]
    got_halo = send_halo(0, pos_ref)

    row = iota((ROWS, ROWS), 0)
    order = (row * 2731) >> 16
    select[...] = one_where((iota((ROWS, ROWS), 1) == row - 3 * order) & (row - PAD * order < TERMS) & (order < TERMS), BF16)
    for ref in (cheb_a, cheb_b, arr_a, arr_b, up1, up2, root, pack_f, tree_e, tree_o, down1, down2, local_box):
        ref[...] = jnp.zeros_like(ref)

    permute = one_where(reversed_digits(iota((BOXES, BOXES), 0)) == iota((BOXES, BOXES), 1), BF16)
    code = mm(permute, (ils_ref[...] + BOXES * ilc_ref[...]).astype(F32).astype(BF16))
    source = reversed_digits(iota((BOXES, BOXES), 1)).astype(F32)
    for kind in range(NCLASS):
        wanted = source + float(BOXES * kind)
        total = jnp.zeros((BOXES, BOXES), F32)
        for entry in range(16):
            total = total + one_where(code[:, entry : entry + 1] == wanted)
        counts_pc[kind * BOXES : (kind + 1) * BOXES, :] = total.astype(BF16)

    def split(value):
        high = rounded(value)
        return high, value - high

    def put_targets(x, y, z):
        rows = []
        halves = [split(v) for v in (x, y, z)]
        rows += [h for h, _ in halves] * 2 + [l for _, l in halves]
        norm = x * x + y * y + z * z
        n1, rest = split(norm)
        n2, n3 = split(rest)
        rows += [n1, n2, n3]
        for index, value in enumerate(rows):
            tgt_f[pl.ds(index, BOXES, stride=16), :] = value

    def put_sources(kind, base, count, coords, weight):
        offset = OFFSETS[kind]
        x, y, z = (v + o if o else v for v, o in zip(coords, offset))
        halves = [split(-2.0 * v) for v in (x, y, z)]
        highs = [h for h, _ in halves]
        m1, rest = split(x * x + y * y + z * z + DELTA_SQ)
        m2, m3 = split(rest)
        ones = jnp.ones_like(x)
        rows = highs + [l for _, l in halves] + highs + [ones] * 3 + [m1, m2, m3, jnp.zeros_like(x)]
        wx, wy, wz = weight
        moments = [wx, wy, wz, wy * z - wz * y, wz * x - wx * z, wx * y - wy * x]
        parts = [split(v) for v in moments]
        zero = jnp.zeros_like(x)
        sums = [h for h, _ in parts] + [zero] * 2 + [l for _, l in parts] + [zero] * 2
        for index in range(16):
            if count == 1:
                spot = slice(base * 16 + index, base * 16 + index + 1)
            else:
                spot = pl.ds(base * 16 + index, count, stride=16)
            src_f[kind, spot, :] = rows[index]
            src_s[kind, spot, :] = sums[index]

    for index in range(12, 16):
        tgt_f[pl.ds(index, BOXES, stride=16), :] = jnp.full((BOXES, SLOTS), 1.0 if index < 15 else 0.0, F32)

    def series(coordinate, put):
        scaled = 0.5 * coordinate
        older, newer = jnp.ones_like(scaled), scaled
        put(0, older)
        put(1, newer)
        for index in range(2, TERMS):
            older, newer = newer, 2.0 * scaled * newer - older
            put(index, newer)

    def own_terms(place):
        x, y, z = place[0], place[1], place[2]
        weight = (weights[0], weights[1], weights[2])
        put_targets(x, y, z)
        put_sources(0, 0, BOXES, (x, y, z), weight)
        put_sources(1, 1, BOXES, (x, y, z), weight)
        put_sources(2, 0, BOXES, (x, y, z), weight)

        def put_a(index, value):
            cheb_a[pl.ds(index, BOXES, stride=PAD), :] = value

        def put_b(index, value):
            cheb_b[pl.ds(index, BOXES, stride=PAD), :] = value

        series(x, put_a)
        series(y, put_b)

    def halo_terms(step):
        for side in range(2):
            got_halo[side].wait_recv()
            if step == 0:
                got_weights[side].wait_recv()
            coords = tuple(halo_p[step, side, c] for c in range(3))
            weight = tuple(halo_w[side, c] for c in range(3))
            put_sources(3 + side, 0, BOXES, coords, weight)
        for side in range(2):
            got_halo[2 + side].wait_recv()
            inside = (g_id > 0) if side == 0 else (g_id < GROUP - 1)
            keep = jnp.where(inside, 1.0, 0.0).astype(F32)
            coords = tuple(end_in[step, side, c : c + 1, :] for c in range(3))
            weight = tuple(end_in[step, side, 3 + c : 4 + c, :] * keep for c in range(3))
            put_sources(1 + side, 0 if side == 0 else BOXES, 1, coords, weight)

    def basis(a_row, b_block, width):
        pieces = []
        for index in range(0, TERMS - 1, 2):
            pair = jnp.concatenate([a_row(index) * b_block, a_row(index + 1) * b_block], axis=0)
            pieces.append(pair.astype(BF16))
        last = jnp.concatenate([a_row(TERMS - 1) * b_block, jnp.zeros((8, width), F32)], axis=0)
        pieces.append(last.astype(BF16))
        return jnp.concatenate(pieces, axis=0)

    def box_order(box):
        return (box % 4) * 16 + ((box // 4) % 4) * 4 + box // 16

    def leaf_one(box):
        start = pl.multiple_of(box * PAD, 8)
        b_block = cheb_b[pl.ds(start, PAD), :]
        phi = basis(lambda j: cheb_a[pl.ds(start + j, 1), :], b_block, SLOTS)
        phi_ref[box] = phi
        lhs = src_s[0, pl.ds(pl.multiple_of(box * 16, 16), 16), :].astype(BF16)
        got = mm_t(lhs, phi)
        got = got[0:8] + got[8:16]
        spot = pl.ds(pl.multiple_of(box_order(box) * 8, 8), 8)
        for t in range(4):
            leaf_box[t, spot, :] = got[:, t * 128 : (t + 1) * 128]

    def arrival_terms():
        got_leave.wait_recv()

        def put_a(index, value):
            arr_a[index : index + 1, :] = value

        def put_b(index, value):
            arr_b[index : index + 1, :] = value

        series(leave_in[0:1, :], put_a)
        series(leave_in[1:2, :], put_b)
        phi = basis(lambda j: arr_a[j : j + 1, :], arr_b[...], CROSS)
        landing = one_where(reversed_digits(iota((BOXES, CROSS), 0)) == arr_ref[...])
        for c in range(3):
            high, low = split(landing * leave_in[3 + c : 4 + c, :])
            arr_leaf[c * BOXES : (c + 1) * BOXES, :] = mm_t(high.astype(BF16), phi) + mm_t(low.astype(BF16), phi)

    def make_leaf():
        for c in range(3):
            rows = slice(c * BOXES, (c + 1) * BOXES)
            for t in range(4):
                lanes = slice(t * 128, (t + 1) * 128)
                own = leaf_box[t, pl.ds(c, BOXES, stride=8), :]
                leaf504[rows, lanes] = (own + arr_leaf[rows, lanes]).astype(BF16)
        leaf441[...] = mm(leaf504[...], select[...]).astype(BF16)

    def pack(value, out):
        root[:, 0:COEF] = value
        for t in range(4):
            pack_f[t * 4 : t * 4 + 3, :] = root[0:3, t * 128 : (t + 1) * 128]
        out[...] = pack_f[...].astype(BF16)

    def upward():
        total = None
        for o in range(4):
            lhs = jnp.concatenate([leaf441[c * BOXES + o * 16 : c * BOXES + o * 16 + 16, 0:COEF] for c in range(3)], axis=0)
            part = mm(lhs, m2m[o])
            total = part if total is None else total + part
        level = rounded(total)
        for o in range(4):
            for c in range(3):
                up1[o, c * 4 : c * 4 + 4, 0:COEF] = level[c * 16 + o * 4 : c * 16 + o * 4 + 4]
        total = None
        for o in range(4):
            part = mm(up1[o, :, 0:COEF].astype(BF16), m2m[o])
            total = part if total is None else total + part
        level = rounded(total)
        for o in range(4):
            for c in range(3):
                up2[o, c : c + 1, 0:COEF] = level[c * 4 + o : c * 4 + o + 1]
        total = None
        for o in range(4):
            part = mm(up2[o, :, 0:COEF].astype(BF16), m2m[o])
            total = part if total is None else total + part
        return total

    def bit(level):
        return (g_id // (1 << level)) % 2

    def spread(index, ref, spot):
        value = ref[index].astype(F32)
        for t in range(4):
            spot[0][spot[1] * 4 : spot[1] * 4 + 4, t * 128 : (t + 1) * 128] = value[t * 4 : t * 4 + 4]

    def tree(step):
        for distance in range(GROUP):
            half = distance // 2
            spot = (half & 1) * 4 + (half >> 1 & 1) * 2 + (half >> 2)
            spread(distance, root_in.at[step], (tree_o if distance & 1 else tree_e, spot))
        lower = tree_e[:, 0:COEF].astype(BF16)
        upper = tree_o[:, 0:COEF].astype(BF16)
        siblings = []
        for level in range(4):
            siblings.append(upper[0:8] if upper.shape[0] >= 8 else upper)
            merged = mm(lower, up[bit(level)]) + mm(upper, up[1 - bit(level)])
            if level < 3:
                half = merged.shape[0] // 2
                lower = merged[0:half].astype(BF16)
                upper = merged[half:].astype(BF16)
        return merged, siblings

    def translate():
        for c in range(3):
            got = mm(counts_pc[...], leaf441[c * BOXES : (c + 1) * BOXES, :]).astype(BF16)
            for kind in range(NCLASS):
                presum[kind, c * BOXES : (c + 1) * BOXES, :] = got[kind * BOXES : (kind + 1) * BOXES]
        total = None
        for kind in range(NCLASS):
            part = mm(presum[kind, :, 0:COEF], m2l[kind])
            total = part if total is None else total + part
        translated[:, 0:COEF] = total

    def near_one(box):
        own = pl.ds(pl.multiple_of(box * 16, 16), 16)
        later = pl.ds(pl.multiple_of(box * 16 + 16, 16), 16)
        spots = [later if kind == 2 else own for kind in range(5)]
        target = tgt_f[own, :].T.astype(BF16)
        features = jnp.concatenate([src_f[kind, spots[kind], :].astype(BF16) for kind in range(5)], axis=1)
        sums = jnp.concatenate([src_s[kind, spots[kind], :].astype(BF16) for kind in range(5)], axis=1)
        inverse = lax.rsqrt(mm(target, features))
        cubed = (inverse * inverse * inverse).astype(BF16)
        total = mm_t(sums, cubed)
        near_box[pl.ds(pl.multiple_of(box * 8, 8), 8), :] = total[0:8] + total[8:16]

    def downward(local):
        local = local.astype(BF16)
        for o in range(4):
            part = rounded(mm_t(local, m2m[o]))
            for c in range(3):
                down1[c * 4 + o : c * 4 + o + 1, 0:COEF] = part[c : c + 1]
        level = down1[:, 0:COEF].astype(BF16)
        for o in range(4):
            part = rounded(mm_t(level, m2m[o]))
            for c in range(3):
                down2[c * 16 + o * 4 : c * 16 + o * 4 + 4, 0:COEF] = part[c * 4 : c * 4 + 4]
        level = down2[:, 0:COEF].astype(BF16)
        for o in range(4):
            part = mm_t(level, m2m[o])
            for c in range(3):
                rows = slice(c * BOXES + o * 16, c * BOXES + o * 16 + 16)
                down3[rows, 0:COEF] = part[c * 16 : c * 16 + 16] + translated[rows, 0:COEF]
        high, low = split(down3[:, 0:COEF])
        chosen = select[:, 0:COEF]
        final = mm_t(high.astype(BF16), chosen) + mm_t(low.astype(BF16), chosen)
        for c in range(3):
            for t in range(4):
                local_box[t, pl.ds(c, BOXES, stride=8), :] = final[c * BOXES : (c + 1) * BOXES, t * 128 : (t + 1) * 128]

    def far_one(box):
        spot = pl.ds(pl.multiple_of(box_order(box) * 8, 8), 8)
        value = jnp.concatenate([local_box[t, spot, :] for t in range(4)], axis=1)
        high, low = split(value)
        lhs = jnp.concatenate([high, low], axis=0).astype(BF16)
        got = mm(lhs, phi_ref[box])
        far_box[pl.ds(pl.multiple_of(box * 8, 8), 8), :] = got[0:8] + got[8:16]

    def boxes(one, first, last, per):
        def body(index, carry):
            for inner in range(per):
                one(first + index * per + inner)
            return carry

        lax.fori_loop(0, (last - first) // per, body, 0)

    for step in range(2):
        place = pos_ref if step == 0 else places
        if step == 1:
            fill_ends(1, places)
            got_halo = send_halo(1, places)
        own_terms(place)
        boxes(leaf_one, 0, BOXES, LEAF_PER)
        if step == 0:
            arrival_terms()
            loads[0].wait()
        make_leaf()
        pack(upward(), root_out.at[step])
        root_in[step, 0] = root_out[step]
        got_roots = [
            remote(root_out.at[step], root_in.at[step, distance], box_peer(distance)) for distance in range(1, GROUP)
        ]
        if step == 0:
            for copy in loads[1:]:
                copy.wait()
        translate()
        halo_terms(step)
        boxes(near_one, 0, BOXES // 2, NEAR_PER)
        for copy in got_roots:
            copy.wait_recv()
        top, siblings = tree(step)
        pack(jnp.concatenate([top, jnp.zeros((4, COEF), F32)], axis=0), sec_out.at[step])
        got_sectors = [
            remote(sec_out.at[step], sec_in.at[step, distance - 1], sector_peer(distance)) for distance in range(1, GROUP)
        ]
        crossed = [mm(siblings[level], tm[bit(level)])[0:4] for level in range(4)]
        boxes(near_one, BOXES // 2, BOXES, NEAR_PER)
        for copy in got_sectors:
            copy.wait_recv()
        total = jnp.zeros((4, COEF), F32)
        for distance in range(1, GROUP):
            spread(distance - 1, sec_in.at[step], (root, 0))
            total = total + mm(root[0:4, 0:COEF].astype(BF16), sec[GROUP - 1 - distance])
        local = total
        for level in reversed(range(4)):
            local = mm_t(local.astype(BF16), up[bit(level)]) + crossed[level]
        downward(local)
        boxes(far_one, 0, BOXES, FAR_PER)
        near = [near_box[pl.ds(c, BOXES, stride=8), :] for c in range(6)]
        x, y, z = place[0], place[1], place[2]
        swept = (
            near[1] * z - near[2] * y - near[3],
            near[2] * x - near[0] * z - near[4],
            near[0] * y - near[1] * x - near[5],
        )
        for c in range(3):
            velocity = INV_FOUR_PI * swept[c] + far_box[pl.ds(c, BOXES, stride=8), :] / float(TERMS)
            if step == 0:
                places[c] = place[c] + TIME_STEP * velocity
            else:
                outp_ref[c] = place[c] + TIME_STEP * velocity
                outv_ref[c] = velocity

    for copy in sends:
        copy.wait_send()


def per_device(positions, strengths, counts, cross_slot, arrive_box, il_source, il_class, m2m, m2l_leaf, tree_up, tree_m2l, m2l_sector):
    vmem = pl.BlockSpec(memory_space=pltpu.VMEM)
    hbm = pl.BlockSpec(memory_space=pl.ANY)
    block = jax.ShapeDtypeStruct((3, BOXES, SLOTS), F32)
    scratch = [
        pltpu.VMEM((4, COEF, COEF), BF16),
        pltpu.VMEM((4, COEF, COEF), BF16),
        pltpu.VMEM((2, COEF, COEF), BF16),
        pltpu.VMEM((2, COEF, COEF), BF16),
        pltpu.VMEM((15, COEF, COEF), BF16),
        pltpu.VMEM((3, BOXES, SLOTS), F32),
        pltpu.VMEM((3, BOXES, SLOTS), F32),
        pltpu.VMEM((2, 2, 3, BOXES, SLOTS), F32),
        pltpu.VMEM((2, 3, BOXES, SLOTS), F32),
        pltpu.VMEM((2, 2, 8, SLOTS), F32),
        pltpu.VMEM((2, 2, 8, SLOTS), F32),
        pltpu.VMEM((8, CROSS), F32),
        pltpu.VMEM((8, CROSS), F32),
        pltpu.VMEM((5, (BOXES + 1) * 16, SLOTS), F32),
        pltpu.VMEM((5, (BOXES + 1) * 16, SLOTS), F32),
        pltpu.VMEM((BOXES * 16, SLOTS), F32),
        pltpu.VMEM((BOXES * PAD, SLOTS), F32),
        pltpu.VMEM((BOXES * PAD, SLOTS), F32),
        pltpu.VMEM((PAD, CROSS), F32),
        pltpu.VMEM((PAD, CROSS), F32),
        pltpu.VMEM((BOXES, ROWS, SLOTS), BF16),
        pltpu.VMEM((4, BOXES * 8, SLOTS), F32),
        pltpu.VMEM((4, BOXES * 8, SLOTS), F32),
        pltpu.VMEM((BOXES * 8, SLOTS), F32),
        pltpu.VMEM((BOXES * 8, SLOTS), F32),
        pltpu.VMEM((3 * BOXES, ROWS), F32),
        pltpu.VMEM((3 * BOXES, ROWS), BF16),
        pltpu.VMEM((3 * BOXES, ROWS), BF16),
        pltpu.VMEM((ROWS, ROWS), BF16),
        pltpu.VMEM((NCLASS * BOXES, BOXES), BF16),
        pltpu.VMEM((NCLASS, 3 * BOXES, ROWS), BF16),
        pltpu.VMEM((3 * BOXES, ROWS), F32),
        pltpu.VMEM((4, 16, ROWS), F32),
        pltpu.VMEM((4, 8, ROWS), F32),
        pltpu.VMEM((8, ROWS), F32),
        pltpu.VMEM((16, SLOTS), F32),
        pltpu.VMEM((2, 16, SLOTS), BF16),
        pltpu.VMEM((2, GROUP, 16, SLOTS), BF16),
        pltpu.VMEM((32, ROWS), F32),
        pltpu.VMEM((32, ROWS), F32),
        pltpu.VMEM((16, ROWS), F32),
        pltpu.VMEM((48, ROWS), F32),
        pltpu.VMEM((3 * BOXES, ROWS), F32),
        pltpu.VMEM((2, 16, SLOTS), BF16),
        pltpu.VMEM((2, GROUP - 1, 16, SLOTS), BF16),
        pltpu.SemaphoreType.DMA((5,)),
        pltpu.SemaphoreType.DMA((72,)),
        pltpu.SemaphoreType.DMA((72,)),
    ]
    new_places, velocity = pl.pallas_call(
        kernel,
        out_shape=(block, block),
        in_specs=[vmem] * 7 + [hbm] * 5,
        out_specs=(vmem, vmem),
        scratch_shapes=scratch,
        compiler_params=pltpu.CompilerParams(
            collective_id=0, has_side_effects=True, vmem_limit_bytes=52 * 1024 * 1024
        ),
        name="vortex_wake",
    )(
        positions[:, 0], strengths[:, 0], counts, cross_slot, arrive_box, il_source[0], il_class[0],
        m2m, m2l_leaf, tree_up, tree_m2l, m2l_sector,
    )
    return new_places[:, None], velocity[:, None]


def solution(mesh):
    placed = (
        P(None, "sector", "box", None),
        P(None, "sector", "box", None),
        P("sector", "box"),
        P("sector", "box"),
        P("sector", "box"),
        P("sector", "box", None),
        P("sector", "box", None),
        P(),
        P(),
        P(),
        P(),
        P(),
    )
    return jax.shard_map(
        per_device,
        mesh=mesh,
        in_specs=placed,
        out_specs=(P(None, "sector", "box", None), P(None, "sector", "box", None)),
        check_vma=False,
    )
```

```python
import functools
import math

import jax
import jax.numpy as jnp
from jax import lax
from jax.experimental import pallas as pl
from jax.experimental.pallas import tpu as pltpu
from jax.sharding import PartitionSpec as P

TERMS = 21
COEF = TERMS * TERMS
PAD = 24
ROWS = 512
BOXES = 64
SLOTS = 128
CROSS = 256
NCLASS = 4
GROUP = 16
LEAF_PER = 16
WAIT_A = 0
TREE_END = 16
WAIT_B = 24
FAR_PER = 16
DELTA_SQ = 0.25
TIME_STEP = 0.02
INV_FOUR_PI = 1.0 / (4.0 * math.pi)
OFFSETS = ((0.0, 0.0, 0.0), (0.0, 0.0, -2.0), (0.0, 0.0, 2.0), (-2.0, 0.0, 0.0), (2.0, 0.0, 0.0))
BF16 = jnp.bfloat16
F32 = jnp.float32
MESH = pl.DeviceIdType.MESH

NN = (((1,), (0,)), ((), ()))
NT = (((1,), (1,)), ((), ()))


def mm(a, b):
    return lax.dot_general(a, b, NN, preferred_element_type=F32)


def mm_t(a, b):
    return lax.dot_general(a, b, NT, preferred_element_type=F32)


def rounded(value):
    return value.astype(BF16).astype(F32)


def iota(shape, dim):
    return lax.broadcasted_iota(jnp.int32, shape, dim)


def one_where(condition, dtype=F32):
    return jnp.where(condition, 1.0, 0.0).astype(dtype)


def reversed_digits(index):
    return (index & 3) * 16 + ((index >> 2) & 3) * 4 + (index >> 4)


def kernel(
    pos_ref, str_ref, cnt_ref, cross_ref, arr_ref, ils_ref, ilc_ref,
    m2m_hbm, m2l_hbm, up_hbm, tm_hbm, sec_hbm,
    outp_ref, outv_ref,
    m2m, m2l, up, tm, sec,
    weights, places, halo_p, halo_w, end_out, end_in, leave_out, leave_in,
    src_f, src_s, tgt_f, cheb_a, cheb_b, arr_a, arr_b, phi_ref,
    leaf_box, local_box, near_box, far_box,
    arr_leaf, leaf504, leaf441, select, counts_pc, presum, translated,
    up1, up2, root, pack_f, root_out, root_in, tree_e, tree_o, down1, down2, down3,
    sec_out, sec_in,
    m2m_t, up_t, select_t, sec_rows,
    load_sem, send_sem, recv_sem,
):
    s_id = lax.axis_index("sector")
    g_id = lax.axis_index("box")

    loads = []
    for index, (src, dst) in enumerate(((m2m_hbm, m2m), (up_hbm, up), (m2l_hbm, m2l), (tm_hbm, tm), (sec_hbm, sec))):
        copy = pltpu.make_async_copy(src, dst, load_sem.at[index])
        copy.start()
        loads.append(copy)

    def box_peer(distance):
        total = 0
        for bit in range(4):
            mine = (g_id // (1 << bit)) % 2
            total = total + ((mine + (distance >> bit & 1)) % 2) * (1 << bit)
        return (s_id, total)

    def sector_peer(distance):
        return ((s_id + distance) % GROUP, g_id)

    barrier = pltpu.get_barrier_semaphore()
    for distance in range(1, GROUP):
        pl.semaphore_signal(barrier, inc=1, device_id=box_peer(distance), device_id_type=MESH)
        pl.semaphore_signal(barrier, inc=1, device_id=sector_peer(distance), device_id_type=MESH)
    before = (s_id, (g_id + GROUP - 1) % GROUP)
    after = (s_id, (g_id + 1) % GROUP)

    next_sem = [0]
    sends = []

    def remote(src, dst, device):
        index = next_sem[0]
        next_sem[0] += 1
        copy = pltpu.make_async_remote_copy(
            src_ref=src, dst_ref=dst, send_sem=send_sem.at[index], recv_sem=recv_sem.at[index],
            device_id=device, device_id_type=MESH,
        )
        copy.start()
        sends.append(copy)
        return copy

    diagonal = iota((BOXES, BOXES), 0) == iota((BOXES, BOXES), 1)
    count_col = jnp.sum(jnp.where(diagonal, jnp.broadcast_to(cnt_ref[...].astype(F32), (BOXES, BOXES)), 0.0), axis=1, keepdims=True)
    present = one_where(iota((BOXES, SLOTS), 1).astype(F32) < count_col)
    crossing = cross_ref[...]
    hit_box = one_where(iota((BOXES, CROSS), 0) == (crossing >> 7), BF16)
    hit_slot = one_where(iota((SLOTS, CROSS), 0) == (crossing & 127))
    departed = mm_t(hit_box, hit_slot.astype(BF16))
    live = present * (1.0 - departed)
    leave_out[...] = jnp.zeros_like(leave_out)
    for c in range(3):
        weights[c] = str_ref[c] * live
    for c in range(6):
        value = pos_ref[c] if c < 3 else str_ref[c - 3] * present
        turned = value.T
        high = turned.astype(BF16)
        rest = turned - high.astype(F32)
        middle = rest.astype(BF16)
        low = (rest - middle.astype(F32)).astype(BF16)
        picked = mm(high, hit_box) + mm(middle, hit_box) + mm(low, hit_box)
        leave_out[c : c + 1, :] = jnp.sum(picked * hit_slot, axis=0, keepdims=True)

    def fill_ends(step, place):
        end_out[step] = jnp.zeros((2, 8, SLOTS), F32)
        for c in range(3):
            end_out[step, 0, c : c + 1, :] = place[c, BOXES - 1 : BOXES, :]
            end_out[step, 1, c : c + 1, :] = place[c, 0:1, :]
            end_out[step, 0, 3 + c : 4 + c, :] = weights[c, BOXES - 1 : BOXES, :]
            end_out[step, 1, 3 + c : 4 + c, :] = weights[c, 0:1, :]

    fill_ends(0, pos_ref)
    pl.semaphore_wait(barrier, 2 * (GROUP - 1))
    got_leave = remote(leave_out, leave_in, sector_peer(1))

    def send_halo(step, place):
        return [
            remote(place, halo_p.at[step, 0], sector_peer(1)),
            remote(place, halo_p.at[step, 1], sector_peer(GROUP - 1)),
            remote(end_out.at[step, 0], end_in.at[step, 0], after),
            remote(end_out.at[step, 1], end_in.at[step, 1], before),
        ]

    got_weights = [
        remote(weights, halo_w.at[0], sector_peer(1)),
        remote(weights, halo_w.at[1], sector_peer(GROUP - 1)),
    ]
    got_halo = send_halo(0, pos_ref)

    row = iota((ROWS, ROWS), 0)
    order = (row * 2731) >> 16
    select[...] = one_where((iota((ROWS, ROWS), 1) == row - 3 * order) & (row - PAD * order < TERMS) & (order < TERMS), BF16)
    wide = iota((COEF, ROWS), 1)
    group = (wide * 2731) >> 16
    select_t[...] = one_where((iota((COEF, ROWS), 0) == wide - 3 * group) & (wide - PAD * group < TERMS) & (group < TERMS), BF16)
    for ref in (cheb_a, cheb_b, arr_a, arr_b, up1, up2, root, pack_f, tree_e, tree_o, down1, down2, local_box):
        ref[...] = jnp.zeros_like(ref)

    permute = one_where(reversed_digits(iota((BOXES, BOXES), 0)) == iota((BOXES, BOXES), 1), BF16)
    code = mm_t(permute, (ils_ref[...] + BOXES * ilc_ref[...]).astype(F32).astype(BF16))
    source = reversed_digits(iota((BOXES, BOXES), 1)).astype(F32)
    for kind in range(NCLASS):
        wanted = source + float(BOXES * kind)
        total = jnp.zeros((BOXES, BOXES), F32)
        for entry in range(16):
            total = total + one_where(code[:, entry : entry + 1] == wanted)
        counts_pc[kind * BOXES : (kind + 1) * BOXES, :] = total.astype(BF16)

    def split(value):
        high = rounded(value)
        return high, value - high

    def put_targets(x, y, z):
        rows = []
        halves = [split(v) for v in (x, y, z)]
        rows += [h for h, _ in halves] * 2 + [l for _, l in halves]
        norm = x * x + y * y + z * z
        n1, rest = split(norm)
        n2, n3 = split(rest)
        rows += [n1, n2, n3]
        for index, value in enumerate(rows):
            tgt_f[pl.ds(index, BOXES, stride=16), :] = value

    def put_sources(kind, base, count, coords, weight, first):
        offset = OFFSETS[kind]
        x, y, z = (v + o if o else v for v, o in zip(coords, offset))
        halves = [split(-2.0 * v) for v in (x, y, z)]
        highs = [h for h, _ in halves]
        m1, rest = split(x * x + y * y + z * z + DELTA_SQ)
        m2, m3 = split(rest)
        ones = jnp.ones_like(x)
        rows = highs + [l for _, l in halves] + highs + [ones] * 3 + [m1, m2, m3, jnp.zeros_like(x)]
        wx, wy, wz = weight
        moments = [wx, wy, wz, wy * z - wz * y, wz * x - wx * z, wx * y - wy * x]
        parts = [split(v) for v in moments]
        zero = jnp.zeros_like(x)
        sums = [h for h, _ in parts] + [zero] * 2 + [l for _, l in parts] + [zero] * 2
        for index in range(16):
            fixed_f = index in (9, 10, 11, 15)
            fixed_s = index % 8 not in (3, 4, 5)
            if count == 1:
                spot = slice(base * 16 + index, base * 16 + index + 1)
            else:
                spot = pl.ds(base * 16 + index, count, stride=16)
            if first or not fixed_f:
                src_f[kind, spot, :] = rows[index]
            if first or not fixed_s:
                src_s[kind, spot, :] = sums[index]

    for index in range(12, 16):
        tgt_f[pl.ds(index, BOXES, stride=16), :] = jnp.full((BOXES, SLOTS), 1.0 if index < 15 else 0.0, F32)

    def series(coordinate, put):
        scaled = 0.5 * coordinate
        older, newer = jnp.ones_like(scaled), scaled
        put(0, older)
        put(1, newer)
        for index in range(2, TERMS):
            older, newer = newer, 2.0 * scaled * newer - older
            put(index, newer)

    def own_terms(step, place):
        x, y, z = place[0], place[1], place[2]
        weight = (weights[0], weights[1], weights[2])
        put_targets(x, y, z)
        put_sources(0, 0, BOXES, (x, y, z), weight, step == 0)
        put_sources(1, 1, BOXES, (x, y, z), weight, step == 0)
        put_sources(2, 0, BOXES, (x, y, z), weight, step == 0)

        def put_a(index, value):
            cheb_a[pl.ds(index, BOXES, stride=PAD), :] = value

        def put_b(index, value):
            cheb_b[pl.ds(index, BOXES, stride=PAD), :] = value

        series(x, put_a)
        series(y, put_b)

    def halo_terms(step):
        for side in range(2):
            got_halo[side].wait_recv()
            if step == 0:
                got_weights[side].wait_recv()
            coords = tuple(halo_p[step, side, c] for c in range(3))
            weight = tuple(halo_w[side, c] for c in range(3))
            put_sources(3 + side, 0, BOXES, coords, weight, step == 0)
        for side in range(2):
            got_halo[2 + side].wait_recv()
            inside = (g_id > 0) if side == 0 else (g_id < GROUP - 1)
            keep = jnp.where(inside, 1.0, 0.0).astype(F32)
            coords = tuple(end_in[step, side, c : c + 1, :] for c in range(3))
            weight = tuple(end_in[step, side, 3 + c : 4 + c, :] * keep for c in range(3))
            put_sources(1 + side, 0 if side == 0 else BOXES, 1, coords, weight, step == 0)

    def basis(a_row, b_block, width):
        pieces = []
        for index in range(0, TERMS - 1, 2):
            pair = jnp.concatenate([a_row(index) * b_block, a_row(index + 1) * b_block], axis=0)
            pieces.append(pair.astype(BF16))
        last = jnp.concatenate([a_row(TERMS - 1) * b_block, jnp.zeros((8, width), F32)], axis=0)
        pieces.append(last.astype(BF16))
        return jnp.concatenate(pieces, axis=0)

    def box_order(box):
        return (box % 4) * 16 + ((box // 4) % 4) * 4 + box // 16

    def leaf_one(box):
        start = pl.multiple_of(box * PAD, 8)
        b_block = cheb_b[pl.ds(start, PAD), :]
        phi = basis(lambda j: cheb_a[pl.ds(start + j, 1), :], b_block, SLOTS)
        phi_ref[box] = phi
        lhs = src_s[0, pl.ds(pl.multiple_of(box * 16, 16), 16), :].astype(BF16)
        got = mm_t(lhs, phi)
        got = got[0:8] + got[8:16]
        spot = pl.ds(pl.multiple_of(box_order(box) * 8, 8), 8)
        for t in range(4):
            leaf_box[t, spot, :] = got[:, t * 128 : (t + 1) * 128]

    def arrival_terms():
        got_leave.wait_recv()

        def put_a(index, value):
            arr_a[index : index + 1, :] = value

        def put_b(index, value):
            arr_b[index : index + 1, :] = value

        series(leave_in[0:1, :], put_a)
        series(leave_in[1:2, :], put_b)
        phi = basis(lambda j: arr_a[j : j + 1, :], arr_b[...], CROSS)
        landing = one_where(reversed_digits(iota((BOXES, CROSS), 0)) == arr_ref[...])
        for c in range(3):
            high, low = split(landing * leave_in[3 + c : 4 + c, :])
            arr_leaf[c * BOXES : (c + 1) * BOXES, :] = mm_t(high.astype(BF16), phi) + mm_t(low.astype(BF16), phi)

    def make_leaf():
        for c in range(3):
            rows = slice(c * BOXES, (c + 1) * BOXES)
            for t in range(4):
                lanes = slice(t * 128, (t + 1) * 128)
                own = leaf_box[t, pl.ds(c, BOXES, stride=8), :]
                leaf504[rows, lanes] = (own + arr_leaf[rows, lanes]).astype(BF16)
        leaf441[...] = mm(leaf504[...], select[...]).astype(BF16)

    def pack(value, out):
        root[:, 0:COEF] = value
        for t in range(4):
            pack_f[t * 4 : t * 4 + 3, :] = root[0:3, t * 128 : (t + 1) * 128]
        out[...] = pack_f[...].astype(BF16)

    def upward():
        total = None
        for o in range(4):
            lhs = jnp.concatenate([leaf441[c * BOXES + o * 16 : c * BOXES + o * 16 + 16, 0:COEF] for c in range(3)], axis=0)
            part = mm(lhs, m2m[o])
            total = part if total is None else total + part
        level = rounded(total)
        for o in range(4):
            for c in range(3):
                up1[o, c * 4 : c * 4 + 4, 0:COEF] = level[c * 16 + o * 4 : c * 16 + o * 4 + 4]
        total = None
        for o in range(4):
            part = mm(up1[o, :, 0:COEF].astype(BF16), m2m[o])
            total = part if total is None else total + part
        level = rounded(total)
        for o in range(4):
            for c in range(3):
                up2[o, c : c + 1, 0:COEF] = level[c * 4 + o : c * 4 + o + 1]
        total = None
        for o in range(4):
            part = mm(up2[o, :, 0:COEF].astype(BF16), m2m[o])
            total = part if total is None else total + part
        return total

    def bit(level):
        return (g_id // (1 << level)) % 2

    def spread(index, ref, spot):
        value = ref[index].astype(F32)
        for t in range(4):
            spot[0][spot[1] * 4 : spot[1] * 4 + 4, t * 128 : (t + 1) * 128] = value[t * 4 : t * 4 + 4]

    def tree(step):
        for distance in range(GROUP):
            half = distance // 2
            spot = (half & 1) * 4 + (half >> 1 & 1) * 2 + (half >> 2)
            spread(distance, root_in.at[step], (tree_o if distance & 1 else tree_e, spot))
        lower = tree_e[:, 0:COEF].astype(BF16)
        upper = tree_o[:, 0:COEF].astype(BF16)
        siblings = []
        for level in range(4):
            siblings.append(upper[0:8] if upper.shape[0] >= 8 else upper)
            merged = mm(lower, up[bit(level)]) + mm(upper, up[1 - bit(level)])
            yield
            if level < 3:
                half = merged.shape[0] // 2
                lower = merged[0:half].astype(BF16)
                upper = merged[half:].astype(BF16)
        return merged, siblings

    def translate():
        for c in range(3):
            got = mm(counts_pc[...], leaf441[c * BOXES : (c + 1) * BOXES, :]).astype(BF16)
            for kind in range(NCLASS):
                presum[kind, c * BOXES : (c + 1) * BOXES, :] = got[kind * BOXES : (kind + 1) * BOXES]
        total = None
        for kind in range(NCLASS):
            part = mm(presum[kind, :, 0:COEF], m2l[kind])
            total = part if total is None else total + part
        translated[:, 0:COEF] = total

    def near_one(box):
        own = pl.ds(pl.multiple_of(box * 16, 16), 16)
        later = pl.ds(pl.multiple_of(box * 16 + 16, 16), 16)
        spots = [later if kind == 2 else own for kind in range(5)]
        target = tgt_f[own, :].T.astype(BF16)
        features = jnp.concatenate([src_f[kind, spots[kind], :].astype(BF16) for kind in range(5)], axis=1)
        sums = jnp.concatenate([src_s[kind, spots[kind], :].astype(BF16) for kind in range(5)], axis=1)
        inverse = lax.rsqrt(mm(target, features))
        cubed = (inverse * inverse * inverse).astype(BF16)
        total = mm_t(sums, cubed)
        near_box[pl.ds(pl.multiple_of(box * 8, 8), 8), :] = total[0:8] + total[8:16]

    def downward(local):
        local = local.astype(BF16)
        for o in range(4):
            part = rounded(mm(local, m2m_t[o]))
            for c in range(3):
                down1[c * 4 + o : c * 4 + o + 1, 0:COEF] = part[c : c + 1]
            yield
        level = down1[:, 0:COEF].astype(BF16)
        for o in range(4):
            part = rounded(mm(level, m2m_t[o]))
            for c in range(3):
                down2[c * 16 + o * 4 : c * 16 + o * 4 + 4, 0:COEF] = part[c * 4 : c * 4 + 4]
            yield
        level = down2[:, 0:COEF].astype(BF16)
        for o in range(4):
            part = mm(level, m2m_t[o])
            for c in range(3):
                rows = slice(c * BOXES + o * 16, c * BOXES + o * 16 + 16)
                down3[rows, 0:COEF] = part[c * 16 : c * 16 + 16] + translated[rows, 0:COEF]
            yield
        for c in range(3):
            high, low = split(down3[c * BOXES : (c + 1) * BOXES, 0:COEF])
            final = mm(high.astype(BF16), select_t[...]) + mm(low.astype(BF16), select_t[...])
            for t in range(4):
                local_box[t, pl.ds(c, BOXES, stride=8), :] = final[:, t * 128 : (t + 1) * 128]
            yield

    def last_chain(step, crossed):
        total = jnp.zeros((4, COEF), F32)
        for distance in range(1, GROUP):
            spread(distance - 1, sec_in.at[step], (sec_rows.at[distance - 1], 0))
            total = total + mm(sec_rows[distance - 1, 0:4, 0:COEF].astype(BF16), sec[GROUP - 1 - distance])
            if distance % 4 == 0:
                yield
        local = total
        for level in reversed(range(4)):
            local = mm(local.astype(BF16), up_t[bit(level)]) + crossed[level]
            yield
        yield from downward(local)

    def interleave(chain, first, last, steps):
        done, result = 0, None
        while True:
            try:
                next(chain)
            except StopIteration as stop:
                result = stop.value
                break
            done += 1
            until = min(last, first + -(-(last - first) * done // steps)) if steps else first
            for box in range(interleave_at[0], until):
                near_one(box)
            interleave_at[0] = max(interleave_at[0], until)
        for box in range(interleave_at[0], last):
            near_one(box)
        return result

    interleave_at = [0]

    def far_one(box):
        spot = pl.ds(pl.multiple_of(box_order(box) * 8, 8), 8)
        value = jnp.concatenate([local_box[t, spot, :] for t in range(4)], axis=1)
        high, low = split(value)
        lhs = jnp.concatenate([high, low], axis=0).astype(BF16)
        got = mm(lhs, phi_ref[box])
        far_box[pl.ds(pl.multiple_of(box * 8, 8), 8), :] = got[0:8] + got[8:16]

    def boxes(one, first, last, per):
        def body(index, carry):
            for inner in range(per):
                one(first + index * per + inner)
            return carry

        lax.fori_loop(0, (last - first) // per, body, 0)

    for step in range(2):
        place = pos_ref if step == 0 else places
        if step == 1:
            fill_ends(1, places)
            got_halo = send_halo(1, places)
        own_terms(step, place)
        boxes(leaf_one, 0, BOXES, LEAF_PER)
        if step == 0:
            arrival_terms()
            loads[0].wait()
        make_leaf()
        pack(upward(), root_out.at[step])
        root_in[step, 0] = root_out[step]
        got_roots = [
            remote(root_out.at[step], root_in.at[step, distance], box_peer(distance)) for distance in range(1, GROUP)
        ]
        if step == 0:
            for copy in loads[1:]:
                copy.wait()
            for index in range(4):
                m2m_t[index] = m2m[index].T
            for index in range(2):
                up_t[index] = up[index].T
        translate()
        halo_terms(step)
        for box in range(0, WAIT_A):
            near_one(box)
        for copy in got_roots:
            copy.wait_recv()
        interleave_at[0] = WAIT_A
        top, siblings = interleave(tree(step), WAIT_A, TREE_END, 4)
        pack(jnp.concatenate([top, jnp.zeros((4, COEF), F32)], axis=0), sec_out.at[step])
        got_sectors = [
            remote(sec_out.at[step], sec_in.at[step, distance - 1], sector_peer(distance)) for distance in range(1, GROUP)
        ]
        crossed = [mm(siblings[level], tm[bit(level)])[0:4] for level in range(4)]
        for box in range(TREE_END, WAIT_B):
            near_one(box)
        for copy in got_sectors:
            copy.wait_recv()
        interleave_at[0] = WAIT_B
        interleave(last_chain(step, crossed), WAIT_B, BOXES, 22)
        boxes(far_one, 0, BOXES, FAR_PER)
        near = [near_box[pl.ds(c, BOXES, stride=8), :] for c in range(6)]
        x, y, z = place[0], place[1], place[2]
        swept = (
            near[1] * z - near[2] * y - near[3],
            near[2] * x - near[0] * z - near[4],
            near[0] * y - near[1] * x - near[5],
        )
        for c in range(3):
            velocity = INV_FOUR_PI * swept[c] + far_box[pl.ds(c, BOXES, stride=8), :] / float(TERMS)
            if step == 0:
                places[c] = place[c] + TIME_STEP * velocity
            else:
                outp_ref[c] = place[c] + TIME_STEP * velocity
                outv_ref[c] = velocity

    for copy in sends:
        copy.wait_send()


def per_device(positions, strengths, counts, cross_slot, arrive_box, il_source, il_class, m2m, m2l_leaf, tree_up, tree_m2l, m2l_sector):
    vmem = pl.BlockSpec(memory_space=pltpu.VMEM)
    hbm = pl.BlockSpec(memory_space=pl.ANY)
    block = jax.ShapeDtypeStruct((3, BOXES, SLOTS), F32)
    scratch = [
        pltpu.VMEM((4, COEF, COEF), BF16),
        pltpu.VMEM((4, COEF, COEF), BF16),
        pltpu.VMEM((2, COEF, COEF), BF16),
        pltpu.VMEM((2, COEF, COEF), BF16),
        pltpu.VMEM((15, COEF, COEF), BF16),
        pltpu.VMEM((3, BOXES, SLOTS), F32),
        pltpu.VMEM((3, BOXES, SLOTS), F32),
        pltpu.VMEM((2, 2, 3, BOXES, SLOTS), F32),
        pltpu.VMEM((2, 3, BOXES, SLOTS), F32),
        pltpu.VMEM((2, 2, 8, SLOTS), F32),
        pltpu.VMEM((2, 2, 8, SLOTS), F32),
        pltpu.VMEM((8, CROSS), F32),
        pltpu.VMEM((8, CROSS), F32),
        pltpu.VMEM((5, (BOXES + 1) * 16, SLOTS), F32),
        pltpu.VMEM((5, (BOXES + 1) * 16, SLOTS), F32),
        pltpu.VMEM((BOXES * 16, SLOTS), F32),
        pltpu.VMEM((BOXES * PAD, SLOTS), F32),
        pltpu.VMEM((BOXES * PAD, SLOTS), F32),
        pltpu.VMEM((PAD, CROSS), F32),
        pltpu.VMEM((PAD, CROSS), F32),
        pltpu.VMEM((BOXES, ROWS, SLOTS), BF16),
        pltpu.VMEM((4, BOXES * 8, SLOTS), F32),
        pltpu.VMEM((4, BOXES * 8, SLOTS), F32),
        pltpu.VMEM((BOXES * 8, SLOTS), F32),
        pltpu.VMEM((BOXES * 8, SLOTS), F32),
        pltpu.VMEM((3 * BOXES, ROWS), F32),
        pltpu.VMEM((3 * BOXES, ROWS), BF16),
        pltpu.VMEM((3 * BOXES, ROWS), BF16),
        pltpu.VMEM((ROWS, ROWS), BF16),
        pltpu.VMEM((NCLASS * BOXES, BOXES), BF16),
        pltpu.VMEM((NCLASS, 3 * BOXES, ROWS), BF16),
        pltpu.VMEM((3 * BOXES, ROWS), F32),
        pltpu.VMEM((4, 16, ROWS), F32),
        pltpu.VMEM((4, 8, ROWS), F32),
        pltpu.VMEM((8, ROWS), F32),
        pltpu.VMEM((16, SLOTS), F32),
        pltpu.VMEM((2, 16, SLOTS), BF16),
        pltpu.VMEM((2, GROUP, 16, SLOTS), BF16),
        pltpu.VMEM((32, ROWS), F32),
        pltpu.VMEM((32, ROWS), F32),
        pltpu.VMEM((16, ROWS), F32),
        pltpu.VMEM((48, ROWS), F32),
        pltpu.VMEM((3 * BOXES, ROWS), F32),
        pltpu.VMEM((2, 16, SLOTS), BF16),
        pltpu.VMEM((2, GROUP - 1, 16, SLOTS), BF16),
        pltpu.VMEM((4, COEF, COEF), BF16),
        pltpu.VMEM((2, COEF, COEF), BF16),
        pltpu.VMEM((COEF, ROWS), BF16),
        pltpu.VMEM((GROUP - 1, 8, ROWS), F32),
        pltpu.SemaphoreType.DMA((5,)),
        pltpu.SemaphoreType.DMA((72,)),
        pltpu.SemaphoreType.DMA((72,)),
    ]
    new_places, velocity = pl.pallas_call(
        kernel,
        out_shape=(block, block),
        in_specs=[vmem] * 7 + [hbm] * 5,
        out_specs=(vmem, vmem),
        scratch_shapes=scratch,
        compiler_params=pltpu.CompilerParams(
            collective_id=0, has_side_effects=True, vmem_limit_bytes=52 * 1024 * 1024
        ),
        name="vortex_wake",
    )(
        positions[:, 0], strengths[:, 0], counts, cross_slot, arrive_box, il_source[0].T, il_class[0].T,
        m2m, m2l_leaf, tree_up, tree_m2l, m2l_sector,
    )
    return new_places[:, None], velocity[:, None]


def solution(mesh):
    placed = (
        P(None, "sector", "box", None),
        P(None, "sector", "box", None),
        P("sector", "box"),
        P("sector", "box"),
        P("sector", "box"),
        P("sector", "box", None),
        P("sector", "box", None),
        P(),
        P(),
        P(),
        P(),
        P(),
    )
    return jax.shard_map(
        per_device,
        mesh=mesh,
        in_specs=placed,
        out_specs=(P(None, "sector", "box", None), P(None, "sector", "box", None)),
        check_vma=False,
    )
```

```python
import functools
import math

import jax
import jax.numpy as jnp
from jax import lax
from jax.experimental import pallas as pl
from jax.experimental.pallas import tpu as pltpu
from jax.sharding import PartitionSpec as P

TERMS = 21
COEF = TERMS * TERMS
PAD = 24
ROWS = 512
BOXES = 64
SLOTS = 128
CROSS = 256
NCLASS = 4
GROUP = 16
BOX_ORDER = (8, 9, 10, 11, 6, 7, 14, 15, 12, 13, 4, 5, 2, 3, 1)
SECTOR_ORDER = (10, 9, 11, 6, 14, 5, 7, 13, 15, 8, 2, 3, 1, 4, 12)
LEAF_PER = 16
NEAR_PER = 8
WAIT_A = 16
TREE_END = 20
WAIT_B = 44
FAR_PER = 16
DELTA_SQ = 0.25
TIME_STEP = 0.02
INV_FOUR_PI = 1.0 / (4.0 * math.pi)
OFFSETS = ((0.0, 0.0, 0.0), (0.0, 0.0, -2.0), (0.0, 0.0, 2.0), (-2.0, 0.0, 0.0), (2.0, 0.0, 0.0))
BF16 = jnp.bfloat16
F32 = jnp.float32
MESH = pl.DeviceIdType.MESH

NN = (((1,), (0,)), ((), ()))
NT = (((1,), (1,)), ((), ()))


def mm(a, b):
    return lax.dot_general(a, b, NN, preferred_element_type=F32)


def mm_t(a, b):
    return lax.dot_general(a, b, NT, preferred_element_type=F32)


def rounded(value):
    return value.astype(BF16).astype(F32)


def iota(shape, dim):
    return lax.broadcasted_iota(jnp.int32, shape, dim)


def one_where(condition, dtype=F32):
    return jnp.where(condition, 1.0, 0.0).astype(dtype)


def reversed_digits(index):
    return (index & 3) * 16 + ((index >> 2) & 3) * 4 + (index >> 4)


def kernel(
    pos_ref, str_ref, cnt_ref, cross_ref, arr_ref, ils_ref, ilc_ref,
    m2m_hbm, m2l_hbm, up_hbm, tm_hbm, sec_hbm,
    outp_ref, outv_ref,
    m2m, m2l, up, tm, sec,
    weights, places, halo_p, halo_w, end_out, end_in, leave_out, leave_in,
    src_f, src_s, tgt_f, cheb_a, cheb_b, arr_a, arr_b, phi_ref,
    leaf_box, local_box, near_box, far_box,
    arr_leaf, leaf504, leaf441, select, counts_pc, presum, translated,
    up1, up2, root, pack_f, root_out, root_in, tree_e, tree_o, down1, down2, down3,
    sec_out, sec_in,
    m2m_t, up_t, select_t, sec_rows,
    load_sem, send_sem, recv_sem,
):
    s_id = lax.axis_index("sector")
    g_id = lax.axis_index("box")

    loads = []
    for index, (src, dst) in enumerate(((m2m_hbm, m2m), (up_hbm, up), (m2l_hbm, m2l), (tm_hbm, tm), (sec_hbm, sec))):
        copy = pltpu.make_async_copy(src, dst, load_sem.at[index])
        copy.start()
        loads.append(copy)

    def box_peer(distance):
        total = 0
        for bit in range(4):
            mine = (g_id // (1 << bit)) % 2
            total = total + ((mine + (distance >> bit & 1)) % 2) * (1 << bit)
        return (s_id, total)

    def sector_peer(distance):
        return ((s_id + distance) % GROUP, g_id)

    barrier = pltpu.get_barrier_semaphore()
    for distance in range(1, GROUP):
        pl.semaphore_signal(barrier, inc=1, device_id=box_peer(BOX_ORDER[distance - 1]), device_id_type=MESH)
        pl.semaphore_signal(barrier, inc=1, device_id=sector_peer(SECTOR_ORDER[distance - 1]), device_id_type=MESH)
    before = (s_id, (g_id + GROUP - 1) % GROUP)
    after = (s_id, (g_id + 1) % GROUP)

    next_sem = [0]
    sends = []

    def remote(src, dst, device):
        index = next_sem[0]
        next_sem[0] += 1
        copy = pltpu.make_async_remote_copy(
            src_ref=src, dst_ref=dst, send_sem=send_sem.at[index], recv_sem=recv_sem.at[index],
            device_id=device, device_id_type=MESH,
        )
        copy.start()
        sends.append(copy)
        return copy

    diagonal = iota((BOXES, BOXES), 0) == iota((BOXES, BOXES), 1)
    count_col = jnp.sum(jnp.where(diagonal, jnp.broadcast_to(cnt_ref[...].astype(F32), (BOXES, BOXES)), 0.0), axis=1, keepdims=True)
    present = one_where(iota((BOXES, SLOTS), 1).astype(F32) < count_col)
    crossing = cross_ref[...]
    hit_box = one_where(iota((BOXES, CROSS), 0) == (crossing >> 7), BF16)
    hit_slot = one_where(iota((SLOTS, CROSS), 0) == (crossing & 127))
    departed = mm_t(hit_box, hit_slot.astype(BF16))
    live = present * (1.0 - departed)
    leave_out[...] = jnp.zeros_like(leave_out)
    for c in range(3):
        weights[c] = str_ref[c] * live
    for c in range(6):
        value = pos_ref[c] if c < 3 else str_ref[c - 3] * present
        turned = value.T
        high = turned.astype(BF16)
        rest = turned - high.astype(F32)
        middle = rest.astype(BF16)
        low = (rest - middle.astype(F32)).astype(BF16)
        picked = mm(high, hit_box) + mm(middle, hit_box) + mm(low, hit_box)
        leave_out[c : c + 1, :] = jnp.sum(picked * hit_slot, axis=0, keepdims=True)

    def fill_ends(step, place):
        end_out[step] = jnp.zeros((2, 8, SLOTS), F32)
        for c in range(3):
            end_out[step, 0, c : c + 1, :] = place[c, BOXES - 1 : BOXES, :]
            end_out[step, 1, c : c + 1, :] = place[c, 0:1, :]
            end_out[step, 0, 3 + c : 4 + c, :] = weights[c, BOXES - 1 : BOXES, :]
            end_out[step, 1, 3 + c : 4 + c, :] = weights[c, 0:1, :]

    def send_halo(step, place):
        return [
            remote(place, halo_p.at[step, 0], sector_peer(1)),
            remote(place, halo_p.at[step, 1], sector_peer(GROUP - 1)),
            remote(end_out.at[step, 0], end_in.at[step, 0], after),
            remote(end_out.at[step, 1], end_in.at[step, 1], before),
        ]

    row = iota((ROWS, ROWS), 0)
    order = (row * 2731) >> 16
    select[...] = one_where((iota((ROWS, ROWS), 1) == row - 3 * order) & (row - PAD * order < TERMS) & (order < TERMS), BF16)
    wide = iota((COEF, ROWS), 1)
    group = (wide * 2731) >> 16
    select_t[...] = one_where((iota((COEF, ROWS), 0) == wide - 3 * group) & (wide - PAD * group < TERMS) & (group < TERMS), BF16)
    for ref in (cheb_a, cheb_b, arr_a, arr_b, up1, up2, root, pack_f, tree_e, tree_o, down1, down2, local_box):
        ref[...] = jnp.zeros_like(ref)

    permute = one_where(reversed_digits(iota((BOXES, BOXES), 0)) == iota((BOXES, BOXES), 1), BF16)
    code = mm_t(permute, (ils_ref[...] + BOXES * ilc_ref[...]).astype(F32).astype(BF16))
    source = reversed_digits(iota((BOXES, BOXES), 1)).astype(F32)
    for kind in range(NCLASS):
        wanted = source + float(BOXES * kind)
        total = jnp.zeros((BOXES, BOXES), F32)
        for entry in range(16):
            total = total + one_where(code[:, entry : entry + 1] == wanted)
        counts_pc[kind * BOXES : (kind + 1) * BOXES, :] = total.astype(BF16)

    def split(value):
        high = rounded(value)
        return high, value - high

    def put_targets(x, y, z):
        rows = []
        halves = [split(v) for v in (x, y, z)]
        rows += [h for h, _ in halves] * 2 + [l for _, l in halves]
        norm = x * x + y * y + z * z
        n1, rest = split(norm)
        n2, n3 = split(rest)
        rows += [n1, n2, n3]
        for index, value in enumerate(rows):
            tgt_f[pl.ds(index, BOXES, stride=16), :] = value

    def put_sources(kind, base, count, coords, weight, first):
        offset = OFFSETS[kind]
        x, y, z = (v + o if o else v for v, o in zip(coords, offset))
        halves = [split(-2.0 * v) for v in (x, y, z)]
        highs = [h for h, _ in halves]
        m1, rest = split(x * x + y * y + z * z + DELTA_SQ)
        m2, m3 = split(rest)
        ones = jnp.ones_like(x)
        rows = highs + [l for _, l in halves] + highs + [ones] * 3 + [m1, m2, m3, jnp.zeros_like(x)]
        wx, wy, wz = weight
        moments = [wx, wy, wz, wy * z - wz * y, wz * x - wx * z, wx * y - wy * x]
        parts = [split(v) for v in moments]
        zero = jnp.zeros_like(x)
        sums = [h for h, _ in parts] + [zero] * 2 + [l for _, l in parts] + [zero] * 2
        for index in range(16):
            fixed_f = index in (9, 10, 11, 15)
            fixed_s = index % 8 not in (3, 4, 5)
            if count == 1:
                spot = slice(base * 16 + index, base * 16 + index + 1)
            else:
                spot = pl.ds(base * 16 + index, count, stride=16)
            if first or not fixed_f:
                src_f[kind, spot, :] = rows[index]
            if first or not fixed_s:
                src_s[kind, spot, :] = sums[index]

    for index in range(12, 16):
        tgt_f[pl.ds(index, BOXES, stride=16), :] = jnp.full((BOXES, SLOTS), 1.0 if index < 15 else 0.0, F32)

    def series(coordinate, put):
        scaled = 0.5 * coordinate
        older, newer = jnp.ones_like(scaled), scaled
        put(0, older)
        put(1, newer)
        for index in range(2, TERMS):
            older, newer = newer, 2.0 * scaled * newer - older
            put(index, newer)

    def own_terms(step, place):
        x, y, z = place[0], place[1], place[2]
        weight = (weights[0], weights[1], weights[2])
        put_targets(x, y, z)
        put_sources(0, 0, BOXES, (x, y, z), weight, step == 0)
        put_sources(1, 1, BOXES, (x, y, z), weight, step == 0)
        put_sources(2, 0, BOXES, (x, y, z), weight, step == 0)

        def put_a(index, value):
            cheb_a[pl.ds(index, BOXES, stride=PAD), :] = value

        def put_b(index, value):
            cheb_b[pl.ds(index, BOXES, stride=PAD), :] = value

        series(x, put_a)
        series(y, put_b)

    def halo_terms(step):
        for side in range(2):
            got_halo[side].wait_recv()
            if step == 0:
                got_weights[side].wait_recv()
            coords = tuple(halo_p[step, side, c] for c in range(3))
            weight = tuple(halo_w[side, c] for c in range(3))
            put_sources(3 + side, 0, BOXES, coords, weight, step == 0)
        for side in range(2):
            got_halo[2 + side].wait_recv()
            inside = (g_id > 0) if side == 0 else (g_id < GROUP - 1)
            keep = jnp.where(inside, 1.0, 0.0).astype(F32)
            coords = tuple(end_in[step, side, c : c + 1, :] for c in range(3))
            weight = tuple(end_in[step, side, 3 + c : 4 + c, :] * keep for c in range(3))
            put_sources(1 + side, 0 if side == 0 else BOXES, 1, coords, weight, step == 0)

    def basis(a_row, b_block, width):
        pieces = []
        for index in range(0, TERMS - 1, 2):
            pair = jnp.concatenate([a_row(index) * b_block, a_row(index + 1) * b_block], axis=0)
            pieces.append(pair.astype(BF16))
        last = jnp.concatenate([a_row(TERMS - 1) * b_block, jnp.zeros((8, width), F32)], axis=0)
        pieces.append(last.astype(BF16))
        return jnp.concatenate(pieces, axis=0)

    def box_order(box):
        return (box % 4) * 16 + ((box // 4) % 4) * 4 + box // 16

    def leaf_one(box):
        start = pl.multiple_of(box * PAD, 8)
        b_block = cheb_b[pl.ds(start, PAD), :]
        phi = basis(lambda j: cheb_a[pl.ds(start + j, 1), :], b_block, SLOTS)
        phi_ref[box] = phi
        lhs = src_s[0, pl.ds(pl.multiple_of(box * 16, 16), 16), :].astype(BF16)
        got = mm_t(lhs, phi)
        got = got[0:8] + got[8:16]
        spot = pl.ds(pl.multiple_of(box_order(box) * 8, 8), 8)
        for t in range(4):
            leaf_box[t, spot, :] = got[:, t * 128 : (t + 1) * 128]

    def arrival_terms():
        got_leave.wait_recv()

        def put_a(index, value):
            arr_a[index : index + 1, :] = value

        def put_b(index, value):
            arr_b[index : index + 1, :] = value

        series(leave_in[0:1, :], put_a)
        series(leave_in[1:2, :], put_b)
        phi = basis(lambda j: arr_a[j : j + 1, :], arr_b[...], CROSS)
        landing = one_where(reversed_digits(iota((BOXES, CROSS), 0)) == arr_ref[...])
        for c in range(3):
            high, low = split(landing * leave_in[3 + c : 4 + c, :])
            arr_leaf[c * BOXES : (c + 1) * BOXES, :] = mm_t(high.astype(BF16), phi) + mm_t(low.astype(BF16), phi)

    def make_leaf():
        for c in range(3):
            rows = slice(c * BOXES, (c + 1) * BOXES)
            for t in range(4):
                lanes = slice(t * 128, (t + 1) * 128)
                own = leaf_box[t, pl.ds(c, BOXES, stride=8), :]
                leaf504[rows, lanes] = (own + arr_leaf[rows, lanes]).astype(BF16)
        leaf441[...] = mm(leaf504[...], select[...]).astype(BF16)

    def pack(value, out):
        root[:, 0:COEF] = value
        for t in range(4):
            pack_f[t * 4 : t * 4 + 3, :] = root[0:3, t * 128 : (t + 1) * 128]
        out[...] = pack_f[...].astype(BF16)

    def upward():
        total = None
        for o in range(4):
            lhs = jnp.concatenate([leaf441[c * BOXES + o * 16 : c * BOXES + o * 16 + 16, 0:COEF] for c in range(3)], axis=0)
            part = mm(lhs, m2m[o])
            total = part if total is None else total + part
        level = rounded(total)
        for o in range(4):
            for c in range(3):
                up1[o, c * 4 : c * 4 + 4, 0:COEF] = level[c * 16 + o * 4 : c * 16 + o * 4 + 4]
        total = None
        for o in range(4):
            part = mm(up1[o, :, 0:COEF].astype(BF16), m2m[o])
            total = part if total is None else total + part
        level = rounded(total)
        for o in range(4):
            for c in range(3):
                up2[o, c : c + 1, 0:COEF] = level[c * 4 + o : c * 4 + o + 1]
        total = None
        for o in range(4):
            part = mm(up2[o, :, 0:COEF].astype(BF16), m2m[o])
            total = part if total is None else total + part
        return total

    def bit(level):
        return (g_id // (1 << level)) % 2

    def spread(index, ref, spot):
        value = ref[index].astype(F32)
        for t in range(4):
            spot[0][spot[1] * 4 : spot[1] * 4 + 4, t * 128 : (t + 1) * 128] = value[t * 4 : t * 4 + 4]

    def tree(step):
        for distance in range(GROUP):
            half = distance // 2
            spot = (half & 1) * 4 + (half >> 1 & 1) * 2 + (half >> 2)
            spread(distance, root_in.at[step], (tree_o if distance & 1 else tree_e, spot))
        lower = tree_e[:, 0:COEF].astype(BF16)
        upper = tree_o[:, 0:COEF].astype(BF16)
        siblings = []
        for level in range(4):
            siblings.append(upper[0:8] if upper.shape[0] >= 8 else upper)
            merged = mm(lower, up[bit(level)]) + mm(upper, up[1 - bit(level)])
            yield
            if level < 3:
                half = merged.shape[0] // 2
                lower = merged[0:half].astype(BF16)
                upper = merged[half:].astype(BF16)
        return merged, siblings

    def translate():
        for c in range(3):
            got = mm(counts_pc[...], leaf441[c * BOXES : (c + 1) * BOXES, :]).astype(BF16)
            for kind in range(NCLASS):
                presum[kind, c * BOXES : (c + 1) * BOXES, :] = got[kind * BOXES : (kind + 1) * BOXES]
        total = None
        for kind in range(NCLASS):
            part = mm(presum[kind, :, 0:COEF], m2l[kind])
            total = part if total is None else total + part
        translated[:, 0:COEF] = total

    def near_one(box):
        own = pl.ds(pl.multiple_of(box * 16, 16), 16)
        later = pl.ds(pl.multiple_of(box * 16 + 16, 16), 16)
        spots = [later if kind == 2 else own for kind in range(5)]
        target = tgt_f[own, :].T.astype(BF16)
        features = jnp.concatenate([src_f[kind, spots[kind], :].astype(BF16) for kind in range(5)], axis=1)
        sums = jnp.concatenate([src_s[kind, spots[kind], :].astype(BF16) for kind in range(5)], axis=1)
        inverse = lax.rsqrt(mm(target, features))
        cubed = (inverse * inverse * inverse).astype(BF16)
        total = mm_t(sums, cubed)
        near_box[pl.ds(pl.multiple_of(box * 8, 8), 8), :] = total[0:8] + total[8:16]

    def downward(local):
        local = local.astype(BF16)
        for o in range(4):
            part = rounded(mm(local, m2m_t[o]))
            for c in range(3):
                down1[c * 4 + o : c * 4 + o + 1, 0:COEF] = part[c : c + 1]
            yield
        level = down1[:, 0:COEF].astype(BF16)
        for o in range(4):
            part = rounded(mm(level, m2m_t[o]))
            for c in range(3):
                down2[c * 16 + o * 4 : c * 16 + o * 4 + 4, 0:COEF] = part[c * 4 : c * 4 + 4]
            yield
        level = down2[:, 0:COEF].astype(BF16)
        for o in range(4):
            part = mm(level, m2m_t[o])
            for c in range(3):
                rows = slice(c * BOXES + o * 16, c * BOXES + o * 16 + 16)
                down3[rows, 0:COEF] = part[c * 16 : c * 16 + 16] + translated[rows, 0:COEF]
            yield
        for c in range(3):
            high, low = split(down3[c * BOXES : (c + 1) * BOXES, 0:COEF])
            final = mm(high.astype(BF16), select_t[...]) + mm(low.astype(BF16), select_t[...])
            for t in range(4):
                local_box[t, pl.ds(c, BOXES, stride=8), :] = final[:, t * 128 : (t + 1) * 128]
            yield

    def last_chain(step, crossed):
        total = jnp.zeros((4, COEF), F32)
        for distance in range(1, GROUP):
            spread(distance - 1, sec_in.at[step], (sec_rows.at[distance - 1], 0))
            total = total + mm(sec_rows[distance - 1, 0:4, 0:COEF].astype(BF16), sec[GROUP - 1 - distance])
            if distance % 4 == 0:
                yield
        local = total
        for level in reversed(range(4)):
            local = mm(local.astype(BF16), up_t[bit(level)]) + crossed[level]
            yield
        yield from downward(local)

    def interleave(chain, first, last, steps):
        done, result = 0, None
        while True:
            try:
                next(chain)
            except StopIteration as stop:
                result = stop.value
                break
            done += 1
            until = min(last, first + -(-(last - first) * done // steps)) if steps else first
            for box in range(interleave_at[0], until):
                near_one(box)
            interleave_at[0] = max(interleave_at[0], until)
        for box in range(interleave_at[0], last):
            near_one(box)
        return result

    interleave_at = [0]

    def far_one(box):
        spot = pl.ds(pl.multiple_of(box_order(box) * 8, 8), 8)
        value = jnp.concatenate([local_box[t, spot, :] for t in range(4)], axis=1)
        high, low = split(value)
        lhs = jnp.concatenate([high, low], axis=0).astype(BF16)
        got = mm(lhs, phi_ref[box])
        far_box[pl.ds(pl.multiple_of(box * 8, 8), 8), :] = got[0:8] + got[8:16]

    def boxes(one, first, last, per):
        def body(index, carry):
            for inner in range(per):
                one(first + index * per + inner)
            return carry

        lax.fori_loop(0, (last - first) // per, body, 0)

    fill_ends(0, pos_ref)
    own_terms(0, pos_ref)
    pl.semaphore_wait(barrier, 2 * (GROUP - 1))
    got_leave = remote(leave_out, leave_in, sector_peer(1))
    got_weights = [
        remote(weights, halo_w.at[0], sector_peer(1)),
        remote(weights, halo_w.at[1], sector_peer(GROUP - 1)),
    ]
    got_halo = send_halo(0, pos_ref)

    for step in range(2):
        place = pos_ref if step == 0 else places
        if step == 1:
            fill_ends(1, places)
            got_halo = send_halo(1, places)
            own_terms(1, places)
        boxes(leaf_one, 0, BOXES, LEAF_PER)
        if step == 0:
            arrival_terms()
            loads[0].wait()
        make_leaf()
        pack(upward(), root_out.at[step])
        root_in[step, 0] = root_out[step]
        got_roots = [
            remote(root_out.at[step], root_in.at[step, distance], box_peer(distance)) for distance in BOX_ORDER
        ]
        if step == 0:
            for copy in loads[1:]:
                copy.wait()
            for index in range(4):
                m2m_t[index] = m2m[index].T
            for index in range(2):
                up_t[index] = up[index].T
        translate()
        halo_terms(step)
        boxes(near_one, 0, WAIT_A, NEAR_PER)
        for copy in got_roots:
            copy.wait_recv()
        interleave_at[0] = WAIT_A
        top, siblings = interleave(tree(step), WAIT_A, TREE_END, 4)
        pack(jnp.concatenate([top, jnp.zeros((4, COEF), F32)], axis=0), sec_out.at[step])
        got_sectors = [
            remote(sec_out.at[step], sec_in.at[step, distance - 1], sector_peer(distance)) for distance in SECTOR_ORDER
        ]
        crossed = [mm(siblings[level], tm[bit(level)])[0:4] for level in range(4)]
        boxes(near_one, TREE_END, WAIT_B, NEAR_PER)
        for copy in got_sectors:
            copy.wait_recv()
        interleave_at[0] = WAIT_B
        interleave(last_chain(step, crossed), WAIT_B, BOXES, 22)
        boxes(far_one, 0, BOXES, FAR_PER)
        near = [near_box[pl.ds(c, BOXES, stride=8), :] for c in range(6)]
        x, y, z = place[0], place[1], place[2]
        swept = (
            near[1] * z - near[2] * y - near[3],
            near[2] * x - near[0] * z - near[4],
            near[0] * y - near[1] * x - near[5],
        )
        for c in range(3):
            velocity = INV_FOUR_PI * swept[c] + far_box[pl.ds(c, BOXES, stride=8), :] / float(TERMS)
            if step == 0:
                places[c] = place[c] + TIME_STEP * velocity
            else:
                outp_ref[c] = place[c] + TIME_STEP * velocity
                outv_ref[c] = velocity

    for copy in sends:
        copy.wait_send()


def per_device(positions, strengths, counts, cross_slot, arrive_box, il_source, il_class, m2m, m2l_leaf, tree_up, tree_m2l, m2l_sector):
    vmem = pl.BlockSpec(memory_space=pltpu.VMEM)
    hbm = pl.BlockSpec(memory_space=pl.ANY)
    block = jax.ShapeDtypeStruct((3, BOXES, SLOTS), F32)
    scratch = [
        pltpu.VMEM((4, COEF, COEF), BF16),
        pltpu.VMEM((4, COEF, COEF), BF16),
        pltpu.VMEM((2, COEF, COEF), BF16),
        pltpu.VMEM((2, COEF, COEF), BF16),
        pltpu.VMEM((15, COEF, COEF), BF16),
        pltpu.VMEM((3, BOXES, SLOTS), F32),
        pltpu.VMEM((3, BOXES, SLOTS), F32),
        pltpu.VMEM((2, 2, 3, BOXES, SLOTS), F32),
        pltpu.VMEM((2, 3, BOXES, SLOTS), F32),
        pltpu.VMEM((2, 2, 8, SLOTS), F32),
        pltpu.VMEM((2, 2, 8, SLOTS), F32),
        pltpu.VMEM((8, CROSS), F32),
        pltpu.VMEM((8, CROSS), F32),
        pltpu.VMEM((5, (BOXES + 1) * 16, SLOTS), F32),
        pltpu.VMEM((5, (BOXES + 1) * 16, SLOTS), F32),
        pltpu.VMEM((BOXES * 16, SLOTS), F32),
        pltpu.VMEM((BOXES * PAD, SLOTS), F32),
        pltpu.VMEM((BOXES * PAD, SLOTS), F32),
        pltpu.VMEM((PAD, CROSS), F32),
        pltpu.VMEM((PAD, CROSS), F32),
        pltpu.VMEM((BOXES, ROWS, SLOTS), BF16),
        pltpu.VMEM((4, BOXES * 8, SLOTS), F32),
        pltpu.VMEM((4, BOXES * 8, SLOTS), F32),
        pltpu.VMEM((BOXES * 8, SLOTS), F32),
        pltpu.VMEM((BOXES * 8, SLOTS), F32),
        pltpu.VMEM((3 * BOXES, ROWS), F32),
        pltpu.VMEM((3 * BOXES, ROWS), BF16),
        pltpu.VMEM((3 * BOXES, ROWS), BF16),
        pltpu.VMEM((ROWS, ROWS), BF16),
        pltpu.VMEM((NCLASS * BOXES, BOXES), BF16),
        pltpu.VMEM((NCLASS, 3 * BOXES, ROWS), BF16),
        pltpu.VMEM((3 * BOXES, ROWS), F32),
        pltpu.VMEM((4, 16, ROWS), F32),
        pltpu.VMEM((4, 8, ROWS), F32),
        pltpu.VMEM((8, ROWS), F32),
        pltpu.VMEM((16, SLOTS), F32),
        pltpu.VMEM((2, 16, SLOTS), BF16),
        pltpu.VMEM((2, GROUP, 16, SLOTS), BF16),
        pltpu.VMEM((32, ROWS), F32),
        pltpu.VMEM((32, ROWS), F32),
        pltpu.VMEM((16, ROWS), F32),
        pltpu.VMEM((48, ROWS), F32),
        pltpu.VMEM((3 * BOXES, ROWS), F32),
        pltpu.VMEM((2, 16, SLOTS), BF16),
        pltpu.VMEM((2, GROUP - 1, 16, SLOTS), BF16),
        pltpu.VMEM((4, COEF, COEF), BF16),
        pltpu.VMEM((2, COEF, COEF), BF16),
        pltpu.VMEM((COEF, ROWS), BF16),
        pltpu.VMEM((GROUP - 1, 8, ROWS), F32),
        pltpu.SemaphoreType.DMA((5,)),
        pltpu.SemaphoreType.DMA((72,)),
        pltpu.SemaphoreType.DMA((72,)),
    ]
    new_places, velocity = pl.pallas_call(
        kernel,
        out_shape=(block, block),
        in_specs=[vmem] * 7 + [hbm] * 5,
        out_specs=(vmem, vmem),
        scratch_shapes=scratch,
        compiler_params=pltpu.CompilerParams(
            collective_id=0, has_side_effects=True, vmem_limit_bytes=52 * 1024 * 1024
        ),
        name="vortex_wake",
    )(
        positions[:, 0], strengths[:, 0], counts, cross_slot, arrive_box, il_source[0].T, il_class[0].T,
        m2m, m2l_leaf, tree_up, tree_m2l, m2l_sector,
    )
    return new_places[:, None], velocity[:, None]


def solution(mesh):
    placed = (
        P(None, "sector", "box", None),
        P(None, "sector", "box", None),
        P("sector", "box"),
        P("sector", "box"),
        P("sector", "box"),
        P("sector", "box", None),
        P("sector", "box", None),
        P(),
        P(),
        P(),
        P(),
        P(),
    )
    return jax.shard_map(
        per_device,
        mesh=mesh,
        in_specs=placed,
        out_specs=(P(None, "sector", "box", None), P(None, "sector", "box", None)),
        check_vma=False,
    )
```

```python
import functools
import math

import jax
import jax.numpy as jnp
from jax import lax
from jax.experimental import pallas as pl
from jax.experimental.pallas import tpu as pltpu
from jax.sharding import PartitionSpec as P

TERMS = 21
COEF = TERMS * TERMS
PAD = 24
ROWS = 512
BOXES = 64
SLOTS = 128
CROSS = 256
NCLASS = 4
GROUP = 16
BOX_ORDER = (8, 9, 10, 11, 6, 7, 14, 15, 12, 13, 4, 5, 2, 3, 1)
SECTOR_ORDER = (10, 9, 11, 6, 14, 5, 7, 13, 15, 8, 2, 3, 1, 4, 12)
LEAF_PER = 16
NEAR_PER = 8
SPLITS = ((16, 20, 44), (12, 16, 40))
FAR_PER = 16
DELTA_SQ = 0.25
TIME_STEP = 0.02
INV_FOUR_PI = 1.0 / (4.0 * math.pi)
OFFSETS = ((0.0, 0.0, 0.0), (0.0, 0.0, -2.0), (0.0, 0.0, 2.0), (-2.0, 0.0, 0.0), (2.0, 0.0, 0.0))
BF16 = jnp.bfloat16
F32 = jnp.float32
MESH = pl.DeviceIdType.MESH

NN = (((1,), (0,)), ((), ()))
NT = (((1,), (1,)), ((), ()))


def mm(a, b):
    return lax.dot_general(a, b, NN, preferred_element_type=F32)


def mm_t(a, b):
    return lax.dot_general(a, b, NT, preferred_element_type=F32)


def rounded(value):
    return value.astype(BF16).astype(F32)


def iota(shape, dim):
    return lax.broadcasted_iota(jnp.int32, shape, dim)


def one_where(condition, dtype=F32):
    return jnp.where(condition, 1.0, 0.0).astype(dtype)


def reversed_digits(index):
    return (index & 3) * 16 + ((index >> 2) & 3) * 4 + (index >> 4)


def kernel(
    pos_ref, str_ref, cnt_ref, cross_ref, arr_ref, ils_ref, ilc_ref,
    m2m_hbm, m2l_hbm, up_hbm, tm_hbm, sec_hbm,
    outp_ref, outv_ref,
    m2m, m2l, up, tm, sec,
    weights, places, halo_p, halo_w, end_out, end_in, leave_out, leave_in,
    src_f, src_s, tgt_f, cheb_a, cheb_b, arr_a, arr_b, phi_ref,
    leaf_box, local_box, near_box, far_box,
    arr_leaf, leaf504, leaf441, select, counts_pc, presum, translated,
    up1, up2, root, pack_f, root_out, root_in, tree_e, tree_o, down1, down2, down3,
    sec_out, sec_in,
    m2m_t, up_t, select_t, sec_rows,
    load_sem, send_sem, recv_sem,
):
    s_id = lax.axis_index("sector")
    g_id = lax.axis_index("box")

    loads = []
    for index, (src, dst) in enumerate(((m2m_hbm, m2m), (up_hbm, up), (m2l_hbm, m2l), (tm_hbm, tm), (sec_hbm, sec))):
        copy = pltpu.make_async_copy(src, dst, load_sem.at[index])
        copy.start()
        loads.append(copy)

    def box_peer(distance):
        total = 0
        for bit in range(4):
            mine = (g_id // (1 << bit)) % 2
            total = total + ((mine + (distance >> bit & 1)) % 2) * (1 << bit)
        return (s_id, total)

    def sector_peer(distance):
        return ((s_id + distance) % GROUP, g_id)

    barrier = pltpu.get_barrier_semaphore()
    for distance in range(1, GROUP):
        pl.semaphore_signal(barrier, inc=1, device_id=box_peer(BOX_ORDER[distance - 1]), device_id_type=MESH)
        pl.semaphore_signal(barrier, inc=1, device_id=sector_peer(SECTOR_ORDER[distance - 1]), device_id_type=MESH)
    before = (s_id, (g_id + GROUP - 1) % GROUP)
    after = (s_id, (g_id + 1) % GROUP)

    next_sem = [0]
    sends = []

    def remote(src, dst, device):
        index = next_sem[0]
        next_sem[0] += 1
        copy = pltpu.make_async_remote_copy(
            src_ref=src, dst_ref=dst, send_sem=send_sem.at[index], recv_sem=recv_sem.at[index],
            device_id=device, device_id_type=MESH,
        )
        copy.start()
        sends.append(copy)
        return copy

    diagonal = iota((BOXES, BOXES), 0) == iota((BOXES, BOXES), 1)
    count_col = jnp.sum(jnp.where(diagonal, jnp.broadcast_to(cnt_ref[...].astype(F32), (BOXES, BOXES)), 0.0), axis=1, keepdims=True)
    present = one_where(iota((BOXES, SLOTS), 1).astype(F32) < count_col)
    crossing = cross_ref[...]
    hit_box = one_where(iota((BOXES, CROSS), 0) == (crossing >> 7), BF16)
    hit_slot = one_where(iota((SLOTS, CROSS), 0) == (crossing & 127))
    departed = mm_t(hit_box, hit_slot.astype(BF16))
    live = present * (1.0 - departed)
    leave_out[...] = jnp.zeros_like(leave_out)
    for c in range(3):
        weights[c] = str_ref[c] * live
    for c in range(6):
        value = pos_ref[c] if c < 3 else str_ref[c - 3] * present
        turned = value.T
        high = turned.astype(BF16)
        rest = turned - high.astype(F32)
        middle = rest.astype(BF16)
        low = (rest - middle.astype(F32)).astype(BF16)
        picked = mm(high, hit_box) + mm(middle, hit_box) + mm(low, hit_box)
        leave_out[c : c + 1, :] = jnp.sum(picked * hit_slot, axis=0, keepdims=True)

    def fill_ends(step, place):
        end_out[step] = jnp.zeros((2, 8, SLOTS), F32)
        for c in range(3):
            end_out[step, 0, c : c + 1, :] = place[c, BOXES - 1 : BOXES, :]
            end_out[step, 1, c : c + 1, :] = place[c, 0:1, :]
            end_out[step, 0, 3 + c : 4 + c, :] = weights[c, BOXES - 1 : BOXES, :]
            end_out[step, 1, 3 + c : 4 + c, :] = weights[c, 0:1, :]

    def send_halo(step, place):
        return [
            remote(place, halo_p.at[step, 0], sector_peer(1)),
            remote(place, halo_p.at[step, 1], sector_peer(GROUP - 1)),
            remote(end_out.at[step, 0], end_in.at[step, 0], after),
            remote(end_out.at[step, 1], end_in.at[step, 1], before),
        ]

    row = iota((ROWS, ROWS), 0)
    order = (row * 2731) >> 16
    select[...] = one_where((iota((ROWS, ROWS), 1) == row - 3 * order) & (row - PAD * order < TERMS) & (order < TERMS), BF16)
    wide = iota((COEF, ROWS), 1)
    group = (wide * 2731) >> 16
    select_t[...] = one_where((iota((COEF, ROWS), 0) == wide - 3 * group) & (wide - PAD * group < TERMS) & (group < TERMS), BF16)
    for ref in (cheb_a, cheb_b, arr_a, arr_b, up1, up2, root, pack_f, tree_e, tree_o, down1, down2, local_box):
        ref[...] = jnp.zeros_like(ref)

    permute = one_where(reversed_digits(iota((BOXES, BOXES), 0)) == iota((BOXES, BOXES), 1), BF16)
    code = mm_t(permute, (ils_ref[...] + BOXES * ilc_ref[...]).astype(F32).astype(BF16))
    source = reversed_digits(iota((BOXES, BOXES), 1)).astype(F32)
    for kind in range(NCLASS):
        wanted = source + float(BOXES * kind)
        total = jnp.zeros((BOXES, BOXES), F32)
        for entry in range(16):
            total = total + one_where(code[:, entry : entry + 1] == wanted)
        counts_pc[kind * BOXES : (kind + 1) * BOXES, :] = total.astype(BF16)

    def split(value):
        high = rounded(value)
        return high, value - high

    def put_targets(x, y, z):
        rows = []
        halves = [split(v) for v in (x, y, z)]
        rows += [h for h, _ in halves] * 2 + [l for _, l in halves]
        norm = x * x + y * y + z * z
        n1, rest = split(norm)
        n2, n3 = split(rest)
        rows += [n1, n2, n3]
        for index, value in enumerate(rows):
            tgt_f[pl.ds(index, BOXES, stride=16), :] = value

    def put_sources(kind, base, count, coords, weight, first):
        offset = OFFSETS[kind]
        x, y, z = (v + o if o else v for v, o in zip(coords, offset))
        halves = [split(-2.0 * v) for v in (x, y, z)]
        highs = [h for h, _ in halves]
        m1, rest = split(x * x + y * y + z * z + DELTA_SQ)
        m2, m3 = split(rest)
        ones = jnp.ones_like(x)
        rows = highs + [l for _, l in halves] + highs + [ones] * 3 + [m1, m2, m3, jnp.zeros_like(x)]
        wx, wy, wz = weight
        moments = [wx, wy, wz, wy * z - wz * y, wz * x - wx * z, wx * y - wy * x]
        parts = [split(v) for v in moments]
        zero = jnp.zeros_like(x)
        sums = [h for h, _ in parts] + [zero] * 2 + [l for _, l in parts] + [zero] * 2
        for index in range(16):
            fixed_f = index in (9, 10, 11, 15)
            fixed_s = index % 8 not in (3, 4, 5)
            if count == 1:
                spot = slice(base * 16 + index, base * 16 + index + 1)
            else:
                spot = pl.ds(base * 16 + index, count, stride=16)
            if first or not fixed_f:
                src_f[kind, spot, :] = rows[index]
            if first or not fixed_s:
                src_s[kind, spot, :] = sums[index]

    for index in range(12, 16):
        tgt_f[pl.ds(index, BOXES, stride=16), :] = jnp.full((BOXES, SLOTS), 1.0 if index < 15 else 0.0, F32)

    def series(coordinate, put):
        scaled = 0.5 * coordinate
        older, newer = jnp.ones_like(scaled), scaled
        put(0, older)
        put(1, newer)
        for index in range(2, TERMS):
            older, newer = newer, 2.0 * scaled * newer - older
            put(index, newer)

    def own_terms(step, place):
        x, y, z = place[0], place[1], place[2]
        weight = (weights[0], weights[1], weights[2])
        put_targets(x, y, z)
        put_sources(0, 0, BOXES, (x, y, z), weight, step == 0)
        put_sources(1, 1, BOXES, (x, y, z), weight, step == 0)
        put_sources(2, 0, BOXES, (x, y, z), weight, step == 0)

    def own_series(place):
        def put_a(index, value):
            cheb_a[pl.ds(index, BOXES, stride=PAD), :] = value

        def put_b(index, value):
            cheb_b[pl.ds(index, BOXES, stride=PAD), :] = value

        series(place[0], put_a)
        series(place[1], put_b)

    def halo_terms(step):
        for side in range(2):
            got_halo[side].wait_recv()
            if step == 0:
                got_weights[side].wait_recv()
            coords = tuple(halo_p[step, side, c] for c in range(3))
            weight = tuple(halo_w[side, c] for c in range(3))
            put_sources(3 + side, 0, BOXES, coords, weight, step == 0)
        for side in range(2):
            got_halo[2 + side].wait_recv()
            inside = (g_id > 0) if side == 0 else (g_id < GROUP - 1)
            keep = jnp.where(inside, 1.0, 0.0).astype(F32)
            coords = tuple(end_in[step, side, c : c + 1, :] for c in range(3))
            weight = tuple(end_in[step, side, 3 + c : 4 + c, :] * keep for c in range(3))
            put_sources(1 + side, 0 if side == 0 else BOXES, 1, coords, weight, step == 0)

    def basis(a_row, b_block, width):
        pieces = []
        for index in range(0, TERMS - 1, 2):
            pair = jnp.concatenate([a_row(index) * b_block, a_row(index + 1) * b_block], axis=0)
            pieces.append(pair.astype(BF16))
        last = jnp.concatenate([a_row(TERMS - 1) * b_block, jnp.zeros((8, width), F32)], axis=0)
        pieces.append(last.astype(BF16))
        return jnp.concatenate(pieces, axis=0)

    def box_order(box):
        return (box % 4) * 16 + ((box // 4) % 4) * 4 + box // 16

    def leaf_one(box):
        start = pl.multiple_of(box * PAD, 8)
        b_block = cheb_b[pl.ds(start, PAD), :]
        phi = basis(lambda j: cheb_a[pl.ds(start + j, 1), :], b_block, SLOTS)
        phi_ref[box] = phi
        lhs = src_s[0, pl.ds(pl.multiple_of(box * 16, 16), 16), :].astype(BF16)
        got = mm_t(lhs, phi)
        got = got[0:8] + got[8:16]
        spot = pl.ds(pl.multiple_of(box_order(box) * 8, 8), 8)
        for t in range(4):
            leaf_box[t, spot, :] = got[:, t * 128 : (t + 1) * 128]

    def arrival_terms():
        got_leave.wait_recv()

        def put_a(index, value):
            arr_a[index : index + 1, :] = value

        def put_b(index, value):
            arr_b[index : index + 1, :] = value

        series(leave_in[0:1, :], put_a)
        series(leave_in[1:2, :], put_b)
        phi = basis(lambda j: arr_a[j : j + 1, :], arr_b[...], CROSS)
        landing = one_where(reversed_digits(iota((BOXES, CROSS), 0)) == arr_ref[...])
        for c in range(3):
            high, low = split(landing * leave_in[3 + c : 4 + c, :])
            arr_leaf[c * BOXES : (c + 1) * BOXES, :] = mm_t(high.astype(BF16), phi) + mm_t(low.astype(BF16), phi)

    def make_leaf():
        for c in range(3):
            rows = slice(c * BOXES, (c + 1) * BOXES)
            for t in range(4):
                lanes = slice(t * 128, (t + 1) * 128)
                own = leaf_box[t, pl.ds(c, BOXES, stride=8), :]
                leaf504[rows, lanes] = (own + arr_leaf[rows, lanes]).astype(BF16)
        leaf441[...] = mm(leaf504[...], select[...]).astype(BF16)

    def pack(value, out):
        root[:, 0:COEF] = value
        for t in range(4):
            pack_f[t * 4 : t * 4 + 3, :] = root[0:3, t * 128 : (t + 1) * 128]
        out[...] = pack_f[...].astype(BF16)

    def upward():
        total = None
        for o in range(4):
            lhs = jnp.concatenate([leaf441[c * BOXES + o * 16 : c * BOXES + o * 16 + 16, 0:COEF] for c in range(3)], axis=0)
            part = mm(lhs, m2m[o])
            total = part if total is None else total + part
        level = rounded(total)
        for o in range(4):
            for c in range(3):
                up1[o, c * 4 : c * 4 + 4, 0:COEF] = level[c * 16 + o * 4 : c * 16 + o * 4 + 4]
        total = None
        for o in range(4):
            part = mm(up1[o, :, 0:COEF].astype(BF16), m2m[o])
            total = part if total is None else total + part
        level = rounded(total)
        for o in range(4):
            for c in range(3):
                up2[o, c : c + 1, 0:COEF] = level[c * 4 + o : c * 4 + o + 1]
        total = None
        for o in range(4):
            part = mm(up2[o, :, 0:COEF].astype(BF16), m2m[o])
            total = part if total is None else total + part
        return total

    def bit(level):
        return (g_id // (1 << level)) % 2

    def spread(index, ref, spot):
        value = ref[index].astype(F32)
        for t in range(4):
            spot[0][spot[1] * 4 : spot[1] * 4 + 4, t * 128 : (t + 1) * 128] = value[t * 4 : t * 4 + 4]

    def tree(step):
        for distance in range(GROUP):
            half = distance // 2
            spot = (half & 1) * 4 + (half >> 1 & 1) * 2 + (half >> 2)
            spread(distance, root_in.at[step], (tree_o if distance & 1 else tree_e, spot))
        lower = tree_e[:, 0:COEF].astype(BF16)
        upper = tree_o[:, 0:COEF].astype(BF16)
        siblings = []
        for level in range(4):
            siblings.append(upper[0:8] if upper.shape[0] >= 8 else upper)
            merged = mm(lower, up[bit(level)]) + mm(upper, up[1 - bit(level)])
            yield
            if level < 3:
                half = merged.shape[0] // 2
                lower = merged[0:half].astype(BF16)
                upper = merged[half:].astype(BF16)
        return merged, siblings

    def translate():
        for c in range(3):
            got = mm(counts_pc[...], leaf441[c * BOXES : (c + 1) * BOXES, :]).astype(BF16)
            for kind in range(NCLASS):
                presum[kind, c * BOXES : (c + 1) * BOXES, :] = got[kind * BOXES : (kind + 1) * BOXES]
        total = None
        for kind in range(NCLASS):
            part = mm(presum[kind, :, 0:COEF], m2l[kind])
            total = part if total is None else total + part
        translated[:, 0:COEF] = total

    def near_one(box):
        own = pl.ds(pl.multiple_of(box * 16, 16), 16)
        later = pl.ds(pl.multiple_of(box * 16 + 16, 16), 16)
        spots = [later if kind == 2 else own for kind in range(5)]
        target = tgt_f[own, :].T.astype(BF16)
        features = jnp.concatenate([src_f[kind, spots[kind], :].astype(BF16) for kind in range(5)], axis=1)
        sums = jnp.concatenate([src_s[kind, spots[kind], :].astype(BF16) for kind in range(5)], axis=1)
        inverse = lax.rsqrt(mm(target, features))
        cubed = (inverse * inverse * inverse).astype(BF16)
        total = mm_t(sums, cubed)
        near_box[pl.ds(pl.multiple_of(box * 8, 8), 8), :] = total[0:8] + total[8:16]

    def downward(local):
        local = local.astype(BF16)
        for o in range(4):
            part = rounded(mm(local, m2m_t[o]))
            for c in range(3):
                down1[c * 4 + o : c * 4 + o + 1, 0:COEF] = part[c : c + 1]
            yield
        level = down1[:, 0:COEF].astype(BF16)
        for o in range(4):
            part = rounded(mm(level, m2m_t[o]))
            for c in range(3):
                down2[c * 16 + o * 4 : c * 16 + o * 4 + 4, 0:COEF] = part[c * 4 : c * 4 + 4]
            yield
        level = down2[:, 0:COEF].astype(BF16)
        for o in range(4):
            part = mm(level, m2m_t[o])
            for c in range(3):
                rows = slice(c * BOXES + o * 16, c * BOXES + o * 16 + 16)
                down3[rows, 0:COEF] = part[c * 16 : c * 16 + 16] + translated[rows, 0:COEF]
            yield
        for c in range(3):
            high, low = split(down3[c * BOXES : (c + 1) * BOXES, 0:COEF])
            final = mm(high.astype(BF16), select_t[...]) + mm(low.astype(BF16), select_t[...])
            for t in range(4):
                local_box[t, pl.ds(c, BOXES, stride=8), :] = final[:, t * 128 : (t + 1) * 128]
            yield

    def last_chain(step, crossed):
        total = jnp.zeros((4, COEF), F32)
        for distance in range(1, GROUP):
            spread(distance - 1, sec_in.at[step], (sec_rows.at[distance - 1], 0))
            total = total + mm(sec_rows[distance - 1, 0:4, 0:COEF].astype(BF16), sec[GROUP - 1 - distance])
            if distance % 4 == 0:
                yield
        local = total
        for level in reversed(range(4)):
            local = mm(local.astype(BF16), up_t[bit(level)]) + crossed[level]
            yield
        yield from downward(local)

    def interleave(chain, first, last, steps):
        done, result = 0, None
        while True:
            try:
                next(chain)
            except StopIteration as stop:
                result = stop.value
                break
            done += 1
            until = min(last, first + -(-(last - first) * done // steps)) if steps else first
            for box in range(interleave_at[0], until):
                near_one(box)
            interleave_at[0] = max(interleave_at[0], until)
        for box in range(interleave_at[0], last):
            near_one(box)
        return result

    interleave_at = [0]

    def far_one(box):
        spot = pl.ds(pl.multiple_of(box_order(box) * 8, 8), 8)
        value = jnp.concatenate([local_box[t, spot, :] for t in range(4)], axis=1)
        high, low = split(value)
        lhs = jnp.concatenate([high, low], axis=0).astype(BF16)
        got = mm(lhs, phi_ref[box])
        far_box[pl.ds(pl.multiple_of(box * 8, 8), 8), :] = got[0:8] + got[8:16]

    def boxes(one, first, last, per):
        def body(index, carry):
            for inner in range(per):
                one(first + index * per + inner)
            return carry

        lax.fori_loop(0, (last - first) // per, body, 0)

    fill_ends(0, pos_ref)
    own_terms(0, pos_ref)
    own_series(pos_ref)
    pl.semaphore_wait(barrier, 2 * (GROUP - 1))
    got_leave = remote(leave_out, leave_in, sector_peer(1))
    got_weights = [
        remote(weights, halo_w.at[0], sector_peer(1)),
        remote(weights, halo_w.at[1], sector_peer(GROUP - 1)),
    ]
    got_halo = send_halo(0, pos_ref)

    for step in range(2):
        place = pos_ref if step == 0 else places
        if step == 1:
            fill_ends(1, places)
            got_halo = send_halo(1, places)
            own_series(places)
        boxes(leaf_one, 0, BOXES, LEAF_PER)
        if step == 0:
            arrival_terms()
            loads[0].wait()
        make_leaf()
        pack(upward(), root_out.at[step])
        root_in[step, 0] = root_out[step]
        got_roots = [
            remote(root_out.at[step], root_in.at[step, distance], box_peer(distance)) for distance in BOX_ORDER
        ]
        if step == 0:
            for copy in loads[1:]:
                copy.wait()
            for index in range(4):
                m2m_t[index] = m2m[index].T
            for index in range(2):
                up_t[index] = up[index].T
        else:
            own_terms(1, places)
        translate()
        halo_terms(step)
        wait_a, tree_end, wait_b = SPLITS[step]
        boxes(near_one, 0, wait_a, NEAR_PER if wait_a % NEAR_PER == 0 else wait_a)
        for copy in got_roots:
            copy.wait_recv()
        interleave_at[0] = wait_a
        top, siblings = interleave(tree(step), wait_a, tree_end, 4)
        pack(jnp.concatenate([top, jnp.zeros((4, COEF), F32)], axis=0), sec_out.at[step])
        got_sectors = [
            remote(sec_out.at[step], sec_in.at[step, distance - 1], sector_peer(distance)) for distance in SECTOR_ORDER
        ]
        crossed = [mm(siblings[level], tm[bit(level)])[0:4] for level in range(4)]
        boxes(near_one, tree_end, wait_b, NEAR_PER)
        for copy in got_sectors:
            copy.wait_recv()
        interleave_at[0] = wait_b
        interleave(last_chain(step, crossed), wait_b, BOXES, 22)
        boxes(far_one, 0, BOXES, FAR_PER)
        near = [near_box[pl.ds(c, BOXES, stride=8), :] for c in range(6)]
        x, y, z = place[0], place[1], place[2]
        swept = (
            near[1] * z - near[2] * y - near[3],
            near[2] * x - near[0] * z - near[4],
            near[0] * y - near[1] * x - near[5],
        )
        for c in range(3):
            velocity = INV_FOUR_PI * swept[c] + far_box[pl.ds(c, BOXES, stride=8), :] / float(TERMS)
            if step == 0:
                places[c] = place[c] + TIME_STEP * velocity
            else:
                outp_ref[c] = place[c] + TIME_STEP * velocity
                outv_ref[c] = velocity

    for copy in sends:
        copy.wait_send()


def per_device(positions, strengths, counts, cross_slot, arrive_box, il_source, il_class, m2m, m2l_leaf, tree_up, tree_m2l, m2l_sector):
    vmem = pl.BlockSpec(memory_space=pltpu.VMEM)
    hbm = pl.BlockSpec(memory_space=pl.ANY)
    block = jax.ShapeDtypeStruct((3, BOXES, SLOTS), F32)
    scratch = [
        pltpu.VMEM((4, COEF, COEF), BF16),
        pltpu.VMEM((4, COEF, COEF), BF16),
        pltpu.VMEM((2, COEF, COEF), BF16),
        pltpu.VMEM((2, COEF, COEF), BF16),
        pltpu.VMEM((15, COEF, COEF), BF16),
        pltpu.VMEM((3, BOXES, SLOTS), F32),
        pltpu.VMEM((3, BOXES, SLOTS), F32),
        pltpu.VMEM((2, 2, 3, BOXES, SLOTS), F32),
        pltpu.VMEM((2, 3, BOXES, SLOTS), F32),
        pltpu.VMEM((2, 2, 8, SLOTS), F32),
        pltpu.VMEM((2, 2, 8, SLOTS), F32),
        pltpu.VMEM((8, CROSS), F32),
        pltpu.VMEM((8, CROSS), F32),
        pltpu.VMEM((5, (BOXES + 1) * 16, SLOTS), F32),
        pltpu.VMEM((5, (BOXES + 1) * 16, SLOTS), F32),
        pltpu.VMEM((BOXES * 16, SLOTS), F32),
        pltpu.VMEM((BOXES * PAD, SLOTS), F32),
        pltpu.VMEM((BOXES * PAD, SLOTS), F32),
        pltpu.VMEM((PAD, CROSS), F32),
        pltpu.VMEM((PAD, CROSS), F32),
        pltpu.VMEM((BOXES, ROWS, SLOTS), BF16),
        pltpu.VMEM((4, BOXES * 8, SLOTS), F32),
        pltpu.VMEM((4, BOXES * 8, SLOTS), F32),
        pltpu.VMEM((BOXES * 8, SLOTS), F32),
        pltpu.VMEM((BOXES * 8, SLOTS), F32),
        pltpu.VMEM((3 * BOXES, ROWS), F32),
        pltpu.VMEM((3 * BOXES, ROWS), BF16),
        pltpu.VMEM((3 * BOXES, ROWS), BF16),
        pltpu.VMEM((ROWS, ROWS), BF16),
        pltpu.VMEM((NCLASS * BOXES, BOXES), BF16),
        pltpu.VMEM((NCLASS, 3 * BOXES, ROWS), BF16),
        pltpu.VMEM((3 * BOXES, ROWS), F32),
        pltpu.VMEM((4, 16, ROWS), F32),
        pltpu.VMEM((4, 8, ROWS), F32),
        pltpu.VMEM((8, ROWS), F32),
        pltpu.VMEM((16, SLOTS), F32),
        pltpu.VMEM((2, 16, SLOTS), BF16),
        pltpu.VMEM((2, GROUP, 16, SLOTS), BF16),
        pltpu.VMEM((32, ROWS), F32),
        pltpu.VMEM((32, ROWS), F32),
        pltpu.VMEM((16, ROWS), F32),
        pltpu.VMEM((48, ROWS), F32),
        pltpu.VMEM((3 * BOXES, ROWS), F32),
        pltpu.VMEM((2, 16, SLOTS), BF16),
        pltpu.VMEM((2, GROUP - 1, 16, SLOTS), BF16),
        pltpu.VMEM((4, COEF, COEF), BF16),
        pltpu.VMEM((2, COEF, COEF), BF16),
        pltpu.VMEM((COEF, ROWS), BF16),
        pltpu.VMEM((GROUP - 1, 8, ROWS), F32),
        pltpu.SemaphoreType.DMA((5,)),
        pltpu.SemaphoreType.DMA((72,)),
        pltpu.SemaphoreType.DMA((72,)),
    ]
    new_places, velocity = pl.pallas_call(
        kernel,
        out_shape=(block, block),
        in_specs=[vmem] * 7 + [hbm] * 5,
        out_specs=(vmem, vmem),
        scratch_shapes=scratch,
        compiler_params=pltpu.CompilerParams(
            collective_id=0, has_side_effects=True, vmem_limit_bytes=52 * 1024 * 1024
        ),
        name="vortex_wake",
    )(
        positions[:, 0], strengths[:, 0], counts, cross_slot, arrive_box, il_source[0].T, il_class[0].T,
        m2m, m2l_leaf, tree_up, tree_m2l, m2l_sector,
    )
    return new_places[:, None], velocity[:, None]


def solution(mesh):
    placed = (
        P(None, "sector", "box", None),
        P(None, "sector", "box", None),
        P("sector", "box"),
        P("sector", "box"),
        P("sector", "box"),
        P("sector", "box", None),
        P("sector", "box", None),
        P(),
        P(),
        P(),
        P(),
        P(),
    )
    return jax.shard_map(
        per_device,
        mesh=mesh,
        in_specs=placed,
        out_specs=(P(None, "sector", "box", None), P(None, "sector", "box", None)),
        check_vma=False,
    )
```
